32 devices in a mesh: dp: 8 (over z, core), seq: 4 (over y, x).
Axes of the slice: x: 2, y: 2, z: 4, core: 2. Of those that a mesh axis runs over, the one named last changes fastest.
Arguments:
- token_ids: int32 [16, 1024], P('dp', 'seq'), may hold values from 0 to 127
- target_ids: int32 [16, 1024], P('dp', 'seq'), may hold values from 0 to 127
- prefix_lengths: int32 [16], P('dp'), may hold values from 128 to 960, as said below
- cluster_ids: int32 [16], P('dp'), may hold values from 0 to 63
- cluster_counts: int32 [64], replicated, may hold values from 1 to 8
- embedding: bfloat16 [128, 2048], P(('dp', 'seq')), may hold values from -0.25 to 0.25
- qkv_weight: bfloat16 [2048, 6144], P(('dp', 'seq')), may hold values from -4 to 4
- out_weight: bfloat16 [2048, 2048], P(('dp', 'seq')), may hold values from -0.375 to 0.375
- norm1_gain: bfloat16 [2048], P(('dp', 'seq')), may hold values from 0.5 to 1.5
- norm1_bias: bfloat16 [2048], P(('dp', 'seq')), may hold values from -1.25 to 1.25
- gate_weight: bfloat16 [2048, 5461], P(('dp', 'seq')), may hold values from -0.125 to 0.125
- up_weight: bfloat16 [2048, 5461], P(('dp', 'seq')), may hold values from -0.125 to 0.125
- down_weight: bfloat16 [2048, 5461], P(('dp', 'seq')), may hold values from -0.4375 to 0.4375
- norm2_gain: bfloat16 [2048], P(('dp', 'seq')), may hold values from 0.5 to 1.5
- norm2_bias: bfloat16 [2048], P(('dp', 'seq')), may hold values from -1.25 to 1.25
Outputs:
- activations: bfloat16 [16, 1024, 2048], P('dp', 'seq')
- input_grad: float32 [16, 1024, 2048], P('dp', 'seq')
- embedding_grad: float32 [128, 2048], P(('dp', 'seq'))
- qkv_grad: float32 [2048, 6144], P(('dp', 'seq'))
- out_grad: float32 [2048, 2048], P(('dp', 'seq'))
- norm1_gain_grad: float32 [2048], P(('dp', 'seq'))
- norm1_bias_grad: float32 [2048], P(('dp', 'seq'))
- gate_grad: float32 [2048, 5461], P(('dp', 'seq'))
- up_grad: float32 [2048, 5461], P(('dp', 'seq'))
- down_grad: float32 [2048, 5461], P(('dp', 'seq'))
- norm2_gain_grad: float32 [2048], P(('dp', 'seq'))
- norm2_bias_grad: float32 [2048], P(('dp', 'seq'))
The draws below stay inside these ranges and needn't reach their ends.
Inputs may be any that keep to these rules, and one draw needn't show every extreme that they name: `prefix_lengths`: one sequence of the batch has a prefix of exactly 960 residues.
All inputs are finite; a program needn't handle non-finite values.
Results may differ from the reference program's by a relative error of at most 0.015.
Values may be sent and summed in bfloat16 or wider, within the bound.
No kernel may reach another device: no remote copies, remote signals or barrier semaphores. Data moves between devices by JAX's collectives and lax.ppermute only.
A program may use at most 448 MiB of HBM per device.

```python
import math
import jax
import jax.numpy as jnp
from jax import lax

D = 2048
HEADS = 16
HEAD = 128
FF = 5461
V = 128
LEN = 1024
CLUSTERS = 64
SEQS = 16


def draw_prefix_lengths(key, part):
    key = jax.random.fold_in(key, 17)
    base_key, pick_key = jax.random.split(key)
    base_lengths = jax.random.randint(base_key, (SEQS,), LEN // 8, LEN - LEN // 16)
    chosen = jax.random.randint(pick_key, (), 0, SEQS)
    longest = jnp.arange(SEQS, dtype=jnp.int32) == chosen
    return jnp.where(longest, LEN - LEN // 16, base_lengths).astype(jnp.int32)


def with_ends(result, key, low, largest):
    spot = [jax.random.randint(jax.random.fold_in(key, axis), (), 0, length) for axis, length in enumerate(result.shape)]
    widest = result.shape.index(max(result.shape))
    beside = spot[:widest] + [(spot[widest] + 1) % result.shape[widest]] + spot[widest + 1:]
    return result.at[tuple(spot)].set(low).at[tuple(beside)].set(largest)


def steps_of(key, dims, cuts, smallest, largest):
    loudness = 1.0
    for position, shards_of in cuts:
        steps = jax.random.uniform(jax.random.fold_in(jax.random.fold_in(key, 6), position), (shards_of,), jnp.float32, smallest / len(cuts), largest / len(cuts))
        loudness = loudness * jnp.repeat(jnp.exp(steps), dims[position] // shards_of).reshape((-1,) + (1,) * (len(dims) - 1 - position))
    return loudness


def normal_values(stream_key, dims, width, most, cuts=(), kind=jnp.bfloat16):
    entries = jax.random.normal(stream_key, dims, jnp.float32) * width
    if len(cuts) > 0:
        entries = steps_of(stream_key, dims, cuts, -0.22, 0.18) * entries
    return jnp.clip(entries, min=-most, max=most).astype(kind)


def setup_inputs(seed: int = 0) -> dict:
    arg_keys = jax.random.split(jax.random.key(seed), 16)
    return {
        "token_ids": with_ends(jax.random.randint(arg_keys[0], (SEQS, LEN), 0, V), jax.random.fold_in(arg_keys[0], 1), 0, V - 1).astype(jnp.int32),
        "target_ids": with_ends(jax.random.randint(arg_keys[1], (SEQS, LEN), 0, V), jax.random.fold_in(arg_keys[1], 1), 0, V - 1).astype(jnp.int32),
        "prefix_lengths": draw_prefix_lengths(jax.random.fold_in(arg_keys[15], 71), 0),
        "cluster_ids": with_ends(jax.random.randint(arg_keys[3], (SEQS,), 0, CLUSTERS), jax.random.fold_in(arg_keys[3], 1), 0, CLUSTERS - 1).astype(jnp.int32),
        "cluster_counts": with_ends(jax.random.randint(arg_keys[4], (CLUSTERS,), 1, 9), jax.random.fold_in(arg_keys[4], 1), 1, 8).astype(jnp.int32),
        "embedding": normal_values(arg_keys[5], (V, D), (D // 4) ** -0.5, 0.25, ((0, 32),)),
        "qkv_weight": normal_values(arg_keys[6], (D, 3 * D), 2 ** -0.5, 4.0, ((0, 32),)),
        "out_weight": normal_values(arg_keys[7], (D, D), (D // 8) ** -0.5, 0.375, ((0, 32),)),
        "norm1_gain": jnp.clip(1.0 + 0.1 * jax.random.normal(arg_keys[8], (D,), jnp.float32), 0.5, 1.5).astype(jnp.bfloat16),
        "norm1_bias": normal_values(arg_keys[9], (D,), 0.2, 1.25, ((0, 32),)),
        "gate_weight": normal_values(arg_keys[10], (D, FF), D ** -0.5, 0.125, ((0, 32),)),
        "up_weight": normal_values(arg_keys[11], (D, FF), D ** -0.5, 0.125, ((0, 32),)),
        "down_weight": normal_values(arg_keys[12], (D, FF), (FF // 32) ** -0.5, 0.4375, ((0, 32),)),
        "norm2_gain": jnp.clip(1.0 + 0.1 * jax.random.normal(arg_keys[13], (D,), jnp.float32), 0.5, 1.5).astype(jnp.bfloat16),
        "norm2_bias": normal_values(arg_keys[14], (D,), 0.2, 1.25, ((0, 32),)),
    }


deep_alpha = math.sqrt(48.0)
loss_scale = 1024.0
norm_epsilon = 1e-05
lookup_scale = 0.1

@jax.custom_vjp
def low(v):
    return lax.optimization_barrier(v.astype(jnp.bfloat16)).astype(jnp.float32)

@jax.custom_vjp
def low_back(v):
    return v

def low_keep(v):
    return (low(v), None)

def low_pass(kept, grad):
    return (grad,)

def back_keep(v):
    return (v, None)

def back_low(kept, grad):
    return (low(grad),)
low.defvjp(low_keep, low_pass)
low_back.defvjp(back_keep, back_low)

def layer_norm(inputs_row, gain_row, bias_row):
    centred = inputs_row - lax.optimization_barrier(jnp.mean(inputs_row, axis=-1, keepdims=True))
    spread_sq = lax.optimization_barrier(jnp.mean(centred * centred, axis=-1, keepdims=True))
    return centred * lax.rsqrt(spread_sq + norm_epsilon) * gain_row + bias_row

def rotary_angles(positions, head_size):
    halves = head_size // 2
    freqs = jnp.power(jnp.float32(10000.0), -2.0 * jnp.arange(halves, dtype=jnp.float32) / head_size)
    return positions.astype(jnp.float32)[:, None] * freqs[None, :]

def rotate(field, angles):
    halves = field.shape[-1] // 2
    cosine = jnp.cos(angles)[:, None, :]
    sine = jnp.sin(angles)[:, None, :]
    first_half = field[..., :halves]
    second_half = field[..., halves:]
    return jnp.concatenate([first_half * cosine - second_half * sine, second_half * cosine + first_half * sine], axis=-1)

def sequence_loss(inputs_seq, prefix, targets, coef_row, params):
    embed_table, qkv_full, out_full, gain_one, bias_one, gate_full, up_full, down_full, gain_two, bias_two = params
    highest = lax.Precision.HIGHEST
    positions = jnp.arange(LEN, dtype=jnp.int32)
    angles = rotary_angles(positions, HEAD)
    qkv_value = low_back(jnp.dot(inputs_seq, qkv_full, precision=highest)).reshape(LEN, 3, HEADS, HEAD)
    queries = low(rotate(qkv_value[:, 0], angles))
    keys_all = low(rotate(qkv_value[:, 1], angles))
    values_all = low(qkv_value[:, 2])
    scores = low_back(jnp.einsum('qhe,khe->hqk', queries, keys_all, precision=highest) * (1.0 / math.sqrt(HEAD)))
    visible = (positions[None, :] < prefix) | (positions[None, :] <= positions[:, None])
    scores = jnp.where(visible[None], scores, -1e+30)
    top_score = lax.optimization_barrier(jnp.max(scores, axis=-1, keepdims=True))
    expo = jnp.exp(scores - top_score)
    probs = low(expo / lax.optimization_barrier(jnp.sum(expo, axis=-1, keepdims=True)))
    context = jnp.einsum('hqk,khe->qhe', probs, values_all, precision=highest).reshape(LEN, HEADS * HEAD)
    context = low_back(low(context))
    attention = low_back(jnp.dot(context, out_full, precision=highest))
    hidden = layer_norm(deep_alpha * inputs_seq + attention, gain_one, bias_one)
    hidden_low = low(hidden)
    gate_value = low_back(jnp.dot(hidden_low, gate_full, precision=highest))
    up_value = low_back(jnp.dot(hidden_low, up_full, precision=highest))
    product = low(jax.nn.gelu(gate_value, approximate=True) * up_value)
    branch = low_back(jnp.dot(product, down_full.T, precision=highest))
    normed = low(layer_norm(deep_alpha * hidden + branch, gain_two, bias_two))
    logits = low_back(jnp.dot(normed, embed_table.T, precision=highest))
    logit_top = lax.optimization_barrier(jnp.max(logits, axis=-1))
    log_total = logit_top + jnp.log(lax.optimization_barrier(jnp.sum(jnp.exp(logits - logit_top[:, None]), axis=-1)))
    vocab_ids = jnp.arange(V, dtype=jnp.int32)
    picked = lax.optimization_barrier(jnp.sum(jnp.where(targets[:, None] == vocab_ids[None, :], logits, 0.0), axis=-1))
    return (jnp.sum((log_total - picked) * coef_row), normed)

def to_float(array):
    return array.astype(jnp.float32)

def reference(token_ids, target_ids, prefix_lengths, cluster_ids, cluster_counts, embedding, qkv_weight, out_weight, norm1_gain, norm1_bias, gate_weight, up_weight, down_weight, norm2_gain, norm2_bias):
    embed_table = to_float(embedding)
    inputs = jnp.take(embed_table, token_ids, axis=0)
    seq_weight = 1.0 / jnp.take(cluster_counts, cluster_ids).astype(jnp.float32)
    positions = jnp.arange(LEN, dtype=jnp.int32)
    counted = (positions[None, :] >= prefix_lengths[:, None]).astype(jnp.float32)
    coefs = loss_scale * seq_weight[:, None] / (LEN - prefix_lengths)[:, None].astype(jnp.float32) * counted
    params = (embed_table, to_float(qkv_weight), to_float(out_weight), to_float(norm1_gain), to_float(norm1_bias), to_float(gate_weight), to_float(up_weight), to_float(down_weight), to_float(norm2_gain), to_float(norm2_bias))

    def forward(inputs_all, weights):
        checked = jax.checkpoint(sequence_loss)

        def step(total, item):
            inputs_seq, prefix, targets, coef_row = item
            loss, normed = checked(inputs_seq, prefix, targets, coef_row, weights)
            return (total + loss, normed)
        total, outputs = lax.scan(step, jnp.float32(0.0), (inputs_all, prefix_lengths, target_ids, coefs))
        return (total, outputs)
    total, pull, outputs = jax.vjp(forward, inputs, params, has_aux=True)
    input_grad, weight_grads = pull(jnp.float32(1.0))
    lookup_grad = jax.ops.segment_sum(input_grad.reshape(-1, D), token_ids.reshape(-1), num_segments=V)
    embedding_grad = lookup_scale * lookup_grad + weight_grads[0]
    return (outputs.astype(jnp.bfloat16), input_grad, embedding_grad, weight_grads[1], weight_grads[2], weight_grads[3], weight_grads[4], weight_grads[5], weight_grads[6], weight_grads[7], weight_grads[8], weight_grads[9])
```

```python
import math

import jax
import jax.numpy as jnp
from jax import lax
from jax.sharding import PartitionSpec as P

HEADS = 16
HEAD = 128
LANES = 128

deep_alpha = math.sqrt(48.0)
loss_scale = 1024.0
norm_epsilon = 1e-05
lookup_scale = 0.1
score_scale = 1.0 / math.sqrt(HEAD)

bf16 = jnp.bfloat16
f32 = jnp.float32
BOTH = ("dp", "seq")
ROWS = (((0,), (0,)), ((), ()))
LAST = (((1,), (1,)), ((), ()))


def dot(left, right, dims=(((1,), (0,)), ((), ()))):
    return lax.dot_general(left, right, dims, preferred_element_type=f32)


def layer_norm(inputs_row, gain_row, bias_row):
    centred = inputs_row - jnp.mean(inputs_row, axis=-1, keepdims=True)
    spread_sq = jnp.mean(centred * centred, axis=-1, keepdims=True)
    return centred * lax.rsqrt(spread_sq + norm_epsilon) * gain_row + bias_row


def rotary_angles(positions, head_size):
    halves = head_size // 2
    freqs = jnp.power(10000.0, -2.0 * jnp.arange(halves, dtype=f32) / head_size)
    return positions.astype(f32)[:, None] * freqs[None, :]


def rotate(field, cosine, sine):
    halves = field.shape[-1] // 2
    first, second = field[..., :halves], field[..., halves:]
    return jnp.concatenate([first * cosine - second * sine, second * cosine + first * sine], axis=-1)


def gated_gelu(gate_in, up_in):
    return jax.nn.gelu(gate_in, approximate=True) * up_in


def exchange(blocks, axes):
    return lax.all_to_all(blocks, axes, split_axis=0, concat_axis=0, tiled=True)


def spread(block, axes):
    count = lax.axis_size(axes)
    return exchange(jnp.broadcast_to(block[None], (count,) + block.shape), axes)


def swap(block, bits):
    return lax.ppermute(block, "seq", [(s, s ^ bits) for s in range(lax.axis_size("seq"))])


def gather_tokens(block):
    if lax.axis_size("seq") != 4:
        return [block] + [swap(block, k) for k in range(1, lax.axis_size("seq"))]
    half = block.shape[0] // 2
    near = swap(block, 1)
    over = swap(block, 2)
    far = jnp.concatenate([swap(near[:half], 2), swap(over[half:], 1)], axis=0)
    return [block, near, over, far]


def scatter_tokens(parts):
    if lax.axis_size("seq") != 4:
        return parts[0] + sum(swap(p.astype(bf16), k).astype(f32) for k, p in enumerate(parts) if k)
    own, near, over, far = parts
    half = own.shape[0] // 2
    far_low = far.astype(bf16)
    by_near = swap(far_low[:half], 1)
    by_over = swap(far_low[half:], 2)
    over = jnp.concatenate([over[:half] + by_near.astype(f32), over[half:]], axis=0)
    near = jnp.concatenate([near[:half], near[half:] + by_over.astype(f32)], axis=0)
    from_over = swap(over.astype(bf16), 2)
    from_near = swap(near.astype(bf16), 1)
    return own + from_over.astype(f32) + from_near.astype(f32)


def on_device(
    token_ids,
    target_ids,
    prefix_lengths,
    cluster_ids,
    cluster_counts,
    embedding,
    qkv_weight,
    out_weight,
    norm1_gain,
    norm1_bias,
    gate_weight,
    up_weight,
    down_weight,
    norm2_gain,
    norm2_bias,
):
    seqs, local_len = token_ids.shape
    count = seqs * local_len
    groups = lax.axis_size("seq")
    dps = lax.axis_size("dp")
    devices = groups * dps
    seq_len = local_len * groups
    my_seq = lax.axis_index("seq")
    my_dp = lax.axis_index("dp")
    positions = my_seq * local_len + jnp.arange(local_len, dtype=jnp.int32)
    rows = qkv_weight.shape[0]
    width = embedding.shape[1]
    vocab_here = embedding.shape[0]
    vocab = vocab_here * devices
    hidden_units = gate_weight.shape[1]
    share = -(-hidden_units // (groups * LANES)) * LANES
    heads_here = HEADS // groups
    head_cols = heads_here * HEAD

    pack = jnp.concatenate(
        [
            embedding.reshape(-1),
            norm1_gain,
            norm1_bias,
            norm2_gain,
            norm2_bias,
            token_ids.reshape(-1).astype(bf16),
        ]
    )
    packs = spread(pack, BOTH)
    table_size = vocab_here * width
    embed_table = packs[:, :table_size].reshape(vocab, width)
    norms = packs[:, table_size : table_size + 4 * rows].reshape(devices, 4, rows)
    norms = norms.transpose(1, 0, 2).reshape(4, width).astype(f32)
    gain_one, bias_one, gain_two, bias_two = norms[0], norms[1], norms[2], norms[3]
    tokens_all = lax.dynamic_slice_in_dim(packs[:, table_size + 4 * rows :], my_dp * groups, groups, 0)
    tokens_all = tokens_all.reshape(groups, seqs, local_len).transpose(1, 0, 2)
    tokens_all = tokens_all.reshape(seqs * seq_len).astype(jnp.int32)
    vocab_ids = jnp.arange(vocab, dtype=jnp.int32)
    token_hot = (token_ids.reshape(count)[:, None] == vocab_ids[None, :]).astype(bf16)
    all_hot = (tokens_all[:, None] == vocab_ids[None, :]).astype(bf16)

    qkv_cols = qkv_weight.reshape(rows, 3, groups, head_cols).transpose(2, 0, 1, 3)
    qkv_cols = exchange(qkv_cols, "seq").reshape(groups * rows, 3 * head_cols)
    out_full = lax.all_gather(out_weight, BOTH, axis=0, tiled=True)

    def columns(weight):
        padded = jnp.pad(weight, ((0, 0), (0, groups * share - hidden_units)))
        return padded.reshape(rows, groups, share).transpose(1, 0, 2)

    ff_cols = jnp.concatenate([columns(gate_weight), columns(up_weight), columns(down_weight)], axis=2)
    ff_cols = exchange(ff_cols, "seq").reshape(groups * rows, 3 * share)
    gate_up_w = lax.all_gather(ff_cols[:, : 2 * share], "dp", axis=0, tiled=True)
    down_w = lax.all_gather(ff_cols[:, 2 * share :], "dp", axis=0, tiled=True)
    qkv_w = lax.all_gather(qkv_cols, "dp", axis=0, tiled=True)

    embed_dp = lax.dynamic_slice_in_dim(embed_table, my_dp * groups * rows, groups * rows, 1)
    qkv_part = dot(embed_dp, qkv_cols).reshape(dps, vocab // dps, 3 * head_cols)
    qkv_rows = jnp.sum(exchange(qkv_part, "dp"), axis=0)
    qkv_high = qkv_rows.astype(bf16)
    qkv_rest = (qkv_rows - qkv_high.astype(f32)).astype(bf16)
    qkv_table = spread(jnp.stack([qkv_high, qkv_rest]), "dp")
    qkv_table = qkv_table.transpose(1, 0, 2, 3).reshape(2 * vocab, 3 * head_cols)
    qkv_value = dot(jnp.concatenate([all_hot, all_hot], axis=1), qkv_table)
    qkv_value = qkv_value.reshape(seqs, seq_len, 3, heads_here, HEAD)
    angles = rotary_angles(jnp.arange(seq_len, dtype=jnp.int32), HEAD)
    cosine, sine = jnp.cos(angles)[:, None, :], jnp.sin(angles)[:, None, :]
    queries = rotate(qkv_value[:, :, 0], cosine, sine).astype(bf16)
    keys = rotate(qkv_value[:, :, 1], cosine, sine).astype(bf16)
    values = qkv_value[:, :, 2].astype(bf16)

    key_pos = jnp.arange(seq_len, dtype=jnp.int32)
    visible = (key_pos[None, None, :] < prefix_lengths[:, None, None]) | (
        key_pos[None, None, :] <= key_pos[None, :, None]
    )
    scores = jnp.einsum("sqhe,skhe->shqk", queries, keys, preferred_element_type=f32) * score_scale
    scores = jnp.where(visible[:, None], scores, -1e30)
    top_score = jnp.max(scores, axis=-1, keepdims=True)
    expo = jnp.exp(scores - top_score)
    probs = expo / jnp.sum(expo, axis=-1, keepdims=True)
    probs_low = probs.astype(bf16)
    context = jnp.einsum("shqk,skhe->sqhe", probs_low, values, preferred_element_type=f32)
    context = context.astype(bf16).reshape(seqs, groups, local_len, head_cols).transpose(1, 0, 2, 3)
    context = exchange(context, "seq").reshape(groups, count, head_cols)
    context = context.transpose(1, 0, 2).reshape(count, width)

    inputs = dot(token_hot, embed_table)
    hidden, norm_one_pull = jax.vjp(
        layer_norm, deep_alpha * inputs + dot(context, out_full), gain_one, bias_one
    )

    hidden_all = jnp.concatenate(gather_tokens(hidden.astype(bf16)), axis=0)
    gate_up = dot(hidden_all, gate_up_w)
    product_full, gelu_pull = jax.vjp(gated_gelu, gate_up[:, :share], gate_up[:, share:])
    product = product_full.astype(bf16)
    branch = scatter_tokens(jnp.split(dot(product, down_w, LAST), groups))
    normed, norm_two_pull = jax.vjp(layer_norm, deep_alpha * hidden + branch, gain_two, bias_two)
    activations = normed.astype(bf16)

    logits = dot(activations, embed_table, LAST)
    cluster_hot = cluster_ids[:, None] == jnp.arange(cluster_counts.shape[0], dtype=jnp.int32)[None, :]
    members = jnp.sum(jnp.where(cluster_hot, cluster_counts[None, :], 0), axis=1).astype(f32)
    counted = (positions[None, :] >= prefix_lengths[:, None]).astype(f32)
    coefs = (
        loss_scale
        * (1.0 / members)[:, None]
        / (seq_len - prefix_lengths)[:, None].astype(f32)
        * counted
    )
    logit_exp = jnp.exp(logits - jnp.max(logits, axis=-1, keepdims=True))
    logit_probs = logit_exp / jnp.sum(logit_exp, axis=-1, keepdims=True)
    target_hot = (target_ids.reshape(count)[:, None] == vocab_ids[None, :]).astype(f32)
    d_logits = (coefs.reshape(count, 1) * (logit_probs - target_hot)).astype(bf16)
    head_grad = dot(d_logits, activations, ROWS)
    d_second, d_gain_two, d_bias_two = norm_two_pull(dot(d_logits, embed_table))

    d_branch = jnp.concatenate(gather_tokens(d_second.astype(bf16)), axis=0)
    d_gate, d_up = gelu_pull(dot(d_branch, down_w))
    d_gate_up = jnp.concatenate([d_gate.astype(bf16), d_up.astype(bf16)], axis=1)
    d_hidden = scatter_tokens(jnp.split(dot(d_gate_up, gate_up_w, LAST), groups))
    d_hidden = d_hidden + deep_alpha * d_second
    down_part = dot(d_branch, product, ROWS).astype(bf16)
    gate_up_part = dot(hidden_all, d_gate_up, ROWS).astype(bf16)

    def own_rows(part, parts):
        mine = lax.psum_scatter(part, "dp", scatter_dimension=0, tiled=True)
        mine = exchange(mine.reshape(groups, rows, parts, share), "seq")
        mine = mine.transpose(2, 1, 0, 3).reshape(parts, rows, groups * share)
        return mine[:, :, :hidden_units].astype(f32)

    (down_grad,) = own_rows(down_part, 1)
    gate_grad, up_grad = own_rows(gate_up_part, 2)

    d_first, d_gain_one, d_bias_one = norm_one_pull(d_hidden)
    d_attention = d_first.astype(bf16)
    out_part = dot(context, d_attention, ROWS).astype(bf16)
    out_grad = lax.psum_scatter(
        lax.psum_scatter(out_part, "dp", scatter_dimension=0, tiled=True),
        "seq",
        scatter_dimension=0,
        tiled=True,
    ).astype(f32)
    d_context = dot(d_attention, out_full, LAST).astype(bf16)
    d_context = d_context.reshape(count, groups, head_cols).transpose(1, 0, 2)
    d_context = exchange(d_context, "seq").reshape(groups, seqs, local_len, head_cols)
    d_context = d_context.transpose(1, 0, 2, 3).reshape(seqs, seq_len, heads_here, HEAD)
    d_probs = jnp.einsum("sqhe,skhe->shqk", d_context, values, preferred_element_type=f32)
    inner = jnp.sum(probs * d_probs, axis=-1, keepdims=True)
    d_scores = (probs * (d_probs - inner)).astype(bf16)
    d_queries = jnp.einsum("shqk,skhe->sqhe", d_scores, keys, preferred_element_type=f32)
    d_keys = jnp.einsum("shqk,sqhe->skhe", d_scores, queries, preferred_element_type=f32)
    d_values = jnp.einsum("shqk,sqhe->skhe", probs_low, d_context, preferred_element_type=f32)
    d_qkv = jnp.stack(
        [
            rotate(d_queries * score_scale, cosine, -sine),
            rotate(d_keys * score_scale, cosine, -sine),
            d_values,
        ],
        axis=2,
    )
    d_qkv = d_qkv.astype(bf16).reshape(seqs * seq_len, 3 * head_cols)

    input_part = dot(d_qkv, qkv_w, LAST).reshape(seqs, groups, local_len, width)
    input_part = input_part.transpose(1, 0, 2, 3).reshape(groups, count, width)
    input_part = exchange(input_part.astype(bf16), "seq")
    input_grad = deep_alpha * d_first + jnp.sum(input_part.astype(f32), axis=0)

    qkv_sums = dot(all_hot, d_qkv, ROWS)
    sums_high = qkv_sums.astype(bf16)
    sums_rest = (qkv_sums - sums_high.astype(f32)).astype(bf16)
    lookup = dot(
        jnp.concatenate([sums_high, sums_rest], axis=1), jnp.concatenate([qkv_w, qkv_w], axis=1), LAST
    )
    lookup_first = lax.dot_general(
        token_hot.astype(f32),
        d_first,
        ROWS,
        precision=lax.Precision.HIGHEST,
        preferred_element_type=f32,
    )
    embed_part = lookup_scale * (lookup + deep_alpha * lookup_first) + head_grad
    norm_part = jnp.stack([d_gain_one, d_bias_one, d_gain_two, d_bias_two])
    norm_part = norm_part.reshape(4, devices, rows).transpose(1, 0, 2).reshape(devices, 4 * rows)
    small = jnp.concatenate([embed_part.reshape(devices, table_size), norm_part], axis=1)
    small = jnp.sum(exchange(small, BOTH), axis=0)
    embedding_grad = small[:table_size].reshape(vocab_here, width)
    norm_grads = small[table_size:].reshape(4, rows)

    sums_mine = jnp.sum(exchange(qkv_sums.reshape(dps, vocab // dps, 3 * head_cols), "dp"), axis=0)
    sums_all = spread(sums_mine.astype(bf16), BOTH)
    sums_all = sums_all.reshape(dps, groups, vocab // dps, 3, head_cols)
    sums_all = sums_all.transpose(0, 2, 3, 1, 4).reshape(vocab, 3 * width)
    embed_rows = lax.dynamic_slice_in_dim(embed_table, (my_dp * groups + my_seq) * rows, rows, 1)
    qkv_grad = dot(embed_rows, sums_all, ROWS)

    return (
        activations.reshape(seqs, local_len, width),
        input_grad.reshape(seqs, local_len, width),
        embedding_grad,
        qkv_grad,
        out_grad,
        norm_grads[0],
        norm_grads[1],
        gate_grad,
        up_grad,
        down_grad,
        norm_grads[2],
        norm_grads[3],
    )


def solution(mesh):
    split = P(BOTH, None)
    line = P(BOTH)
    return jax.shard_map(
        on_device,
        mesh=mesh,
        in_specs=(
            P("dp", "seq"),
            P("dp", "seq"),
            P("dp"),
            P("dp"),
            P(),
            split,
            split,
            split,
            line,
            line,
            split,
            split,
            split,
            line,
            line,
        ),
        out_specs=(
            P("dp", "seq", None),
            P("dp", "seq", None),
            split,
            split,
            split,
            line,
            line,
            split,
            split,
            split,
            line,
            line,
        ),
        check_vma=False,
    )
```

```python
import math

import jax
import jax.numpy as jnp
from jax import lax
from jax.experimental import pallas as pl
from jax.experimental.pallas import tpu as pltpu
from jax.sharding import PartitionSpec as P

HEADS = 16
HEAD = 128
LANES = 128

deep_alpha = math.sqrt(48.0)
loss_scale = 1024.0
norm_epsilon = 1e-05
lookup_scale = 0.1
score_scale = 1.0 / math.sqrt(HEAD)
LOG2_E = math.log2(math.e)

bf16 = jnp.bfloat16
f32 = jnp.float32
BOTH = ("dp", "seq")
ROWS = (((0,), (0,)), ((), ()))
LAST = (((1,), (1,)), ((), ()))


def dot(left, right, dims=(((1,), (0,)), ((), ()))):
    return lax.dot_general(left, right, dims, preferred_element_type=f32)


def layer_norm(inputs_row, gain_row, bias_row):
    centred = inputs_row - jnp.mean(inputs_row, axis=-1, keepdims=True)
    spread_sq = jnp.mean(centred * centred, axis=-1, keepdims=True)
    return centred * lax.rsqrt(spread_sq + norm_epsilon) * gain_row + bias_row


def rotary_angles(positions, head_size):
    halves = head_size // 2
    freqs = jnp.power(10000.0, -2.0 * jnp.arange(halves, dtype=f32) / head_size)
    return positions.astype(f32)[:, None] * freqs[None, :]


def rotate(field, cosine, sine):
    halves = field.shape[-1] // 2
    first, second = field[..., :halves], field[..., halves:]
    return jnp.concatenate([first * cosine - second * sine, second * cosine + first * sine], axis=-1)


def gated_gelu(gate, up):
    root = math.sqrt(2.0 / math.pi)
    square = gate * gate
    bend = jnp.tanh(gate * (root + (root * 0.044715) * square))
    half = 0.5 + 0.5 * bend
    gelu = gate * half
    slope = half + gate * (0.5 - 0.5 * bend * bend) * (root + (3.0 * root * 0.044715) * square)
    return gelu * up, slope * up, gelu


def halves(value):
    high = lax.reduce_precision(value, 8, 7)
    return jnp.stack([high.astype(bf16), (value - high).astype(bf16)])


def together(*values):
    return lax.optimization_barrier(values)


def exchange(blocks, axes):
    return lax.all_to_all(blocks, axes, split_axis=0, concat_axis=0, tiled=True)


def spread(block, axes):
    count = lax.axis_size(axes)
    return exchange(jnp.broadcast_to(block[None], (count,) + block.shape), axes)


def swap(block, bits):
    return lax.ppermute(block, "seq", [(s, s ^ bits) for s in range(lax.axis_size("seq"))])


def swap_dp(block, bits):
    return lax.ppermute(block, "dp", [(d, d ^ bits) for d in range(lax.axis_size("dp"))])


def place(axis):
    return lax.axis_index(axis).astype(jnp.int32).reshape(1)


def take_columns(weight, groups, pieces, size):
    rows, columns = weight.shape

    def kernel(place_ref, weight_ref, out_ref):
        for g in range(groups):
            for i in range(pieces):
                first = (i * groups + g) * size
                block = weight_ref[:, first : min(first + size, columns)]
                if block.shape[1] < size:
                    rest = jnp.zeros((rows, size - block.shape[1]), block.dtype)
                    block = jnp.concatenate([block, rest], axis=1)
                out_ref[lax.bitwise_xor(place_ref[0], g), :, i * size : (i + 1) * size] = block

    return pl.pallas_call(
        kernel,
        in_specs=[pl.BlockSpec(memory_space=pltpu.SMEM), pl.BlockSpec(memory_space=pltpu.VMEM)],
        out_specs=pl.BlockSpec(memory_space=pltpu.VMEM),
        out_shape=jax.ShapeDtypeStruct((groups, rows, pieces * size), weight.dtype),
        compiler_params=pltpu.CompilerParams(vmem_limit_bytes=16 << 20),
    )(place("seq"), weight)


def swap_all(blocks):
    return [blocks[0]] + [swap(blocks[k], k) for k in range(1, blocks.shape[0])]


def join_rows(blocks):
    rows, columns = blocks[0].shape
    groups = len(blocks)

    def kernel(place_ref, *refs):
        for k in range(groups):
            first = pl.multiple_of(lax.bitwise_xor(place_ref[0], k) * rows, rows)
            refs[-1][pl.ds(first, rows), :] = refs[k][...]

    return pl.pallas_call(
        kernel,
        in_specs=[pl.BlockSpec(memory_space=pltpu.SMEM)] + [pl.BlockSpec(memory_space=pltpu.VMEM)] * groups,
        out_specs=pl.BlockSpec(memory_space=pltpu.VMEM),
        out_shape=jax.ShapeDtypeStruct((groups * rows, columns), blocks[0].dtype),
        compiler_params=pltpu.CompilerParams(vmem_limit_bytes=16 << 20),
    )(place("seq"), *blocks)


def take_rows(field, groups):
    rows, columns = field.shape[0] // groups, field.shape[1]

    def kernel(place_ref, field_ref, out_ref):
        for g in range(groups):
            out_ref[lax.bitwise_xor(place_ref[0], g)] = field_ref[g * rows : (g + 1) * rows]

    return pl.pallas_call(
        kernel,
        in_specs=[pl.BlockSpec(memory_space=pltpu.SMEM), pl.BlockSpec(memory_space=pltpu.VMEM)],
        out_specs=pl.BlockSpec(memory_space=pltpu.VMEM),
        out_shape=jax.ShapeDtypeStruct((groups, rows, columns), field.dtype),
        compiler_params=pltpu.CompilerParams(vmem_limit_bytes=16 << 20),
    )(place("seq"), field)


def join_columns(blocks, columns):
    rows, size = blocks[0].shape
    groups = len(blocks)

    def kernel(place_ref, *refs):
        for g in range(groups):
            source = lax.bitwise_xor(place_ref[0], g)
            block = refs[0][...]
            for k in range(1, groups):
                block = jnp.where(source == k, refs[k][...], block)
            end = min((g + 1) * size, columns)
            refs[-1][:, g * size : end] = block[:, : end - g * size].astype(f32)

    return pl.pallas_call(
        kernel,
        in_specs=[pl.BlockSpec(memory_space=pltpu.SMEM)] + [pl.BlockSpec(memory_space=pltpu.VMEM)] * groups,
        out_specs=pl.BlockSpec(memory_space=pltpu.VMEM),
        out_shape=jax.ShapeDtypeStruct((rows, columns), f32),
        compiler_params=pltpu.CompilerParams(vmem_limit_bytes=16 << 20),
    )(place("seq"), *blocks)


def table_grad(sums, embed_rows):
    dps, groups, piece, columns = sums.shape
    size = columns // 3
    rows = embed_rows.shape[1]

    def kernel(sums_ref, embed_ref, out_ref):
        embed = embed_ref[...]
        for i in range(3):
            for g in range(groups):
                block = sums_ref[:, g, :, i * size : (i + 1) * size].reshape(dps * piece, size)
                first = (i * groups + g) * size
                out_ref[:, first : first + size] = dot(embed, block, ROWS)

    return pl.pallas_call(
        kernel,
        in_specs=[pl.BlockSpec(memory_space=pltpu.VMEM)] * 2,
        out_specs=pl.BlockSpec(memory_space=pltpu.VMEM),
        out_shape=jax.ShapeDtypeStruct((rows, 3 * groups * size), f32),
        compiler_params=pltpu.CompilerParams(vmem_limit_bytes=24 << 20),
    )(sums, embed_rows)


def join_out(mine, other):
    groups, chips, rows, width = mine.shape

    def kernel(seq_ref, dp_ref, mine_ref, other_ref, out_ref):
        chip = dp_ref[0] // 2
        for source, ref in enumerate((mine_ref, other_ref)):

            @pl.when(pl.program_id(0) == source)
            def _(ref=ref):
                for j in range(chips):
                    out_ref[lax.bitwise_xor(chip, j), 0, 0] = ref[0, j]

    last = groups - 1
    return pl.pallas_call(
        kernel,
        grid_spec=pltpu.PrefetchScalarGridSpec(
            num_scalar_prefetch=2,
            grid=(2, groups),
            in_specs=[
                pl.BlockSpec((1, chips, rows, width), lambda a, k, at, dp: (jnp.where(a == 0, k, last), 0, 0, 0)),
                pl.BlockSpec((1, chips, rows, width), lambda a, k, at, dp: (jnp.where(a == 0, 0, k), 0, 0, 0)),
            ],
            out_specs=pl.BlockSpec(
                (chips, 1, 1, rows, width),
                lambda a, k, at, dp: (
                    0,
                    lax.bitwise_xor(lax.rem(dp[0], 2), a),
                    lax.bitwise_xor(at[0], k),
                    0,
                    0,
                ),
            ),
        ),
        out_shape=jax.ShapeDtypeStruct((chips, 2, groups, rows, width), mine.dtype),
        compiler_params=pltpu.CompilerParams(vmem_limit_bytes=24 << 20),
    )(place("seq"), place("dp"), mine, other).reshape(chips * 2 * groups * rows, width)


def sum_dp(parts):
    kept = parts[0] + swap_dp(parts[1], 1)
    return kept[0] + sum(swap_dp(kept[j], 2 * j) for j in range(1, kept.shape[0]))


def spread_dp(block):
    blocks = jnp.stack([block] + [swap_dp(block, 2 * j) for j in range(1, lax.axis_size("dp") // 2)])
    return jnp.stack([blocks, swap_dp(blocks, 1)]), blocks


def gather_tokens(block, work):
    if lax.axis_size("seq") != 4:
        blocks = [block] + [swap(block, k) for k in range(1, lax.axis_size("seq"))]
        return blocks, [work(k, b) for k, b in enumerate(blocks)]
    half = block.shape[0] // 2
    near = swap(block, 1)
    over = swap(block, 2)
    own_work = work(0, block)
    near, over, own_work = together(near, over, own_work)
    far_one = swap(near[:half], 2)
    far_two = swap(over[half:], 1)
    near_work, over_work = work(1, near), work(2, over)
    far_one, far_two, near_work, over_work = together(far_one, far_two, near_work, over_work)
    far = jnp.concatenate([far_one, far_two], axis=0)
    return [block, near, over, far], [own_work, near_work, over_work, work(3, far)]


def gather_blocks(block, held):
    if lax.axis_size("seq") != 4:
        return jnp.stack([block] + [swap(block, k) for k in range(1, lax.axis_size("seq"))])
    half = block.shape[0] // 2
    near, over = swap(block, 1), swap(block, 2)
    near_held, over_held, _ = together(near, over, held)
    far = jnp.concatenate([swap(near_held[:half], 2), swap(over_held[half:], 1)], axis=0)
    return jnp.stack([block, near, over, far])


def scatter_tokens(part, first=None, last=None, first_given=(), last_given=()):
    if lax.axis_size("seq") != 4:
        total = part(0).astype(f32)
        for k in range(1, lax.axis_size("seq")):
            total = total + swap(part(k).astype(bf16), k).astype(f32)
        return total, first and first(*first_given), last and last(*last_given)
    far = part(3).astype(bf16)
    half = far.shape[0] // 2
    far, *first_given = together(far, *first_given)
    by_near = swap(far[:half], 1)
    by_over = swap(far[half:], 2)
    first_done = first(*first_given) if first else ()
    by_near, by_over, near, over, own, first_done = together(
        by_near, by_over, part(1), part(2), part(0), first_done
    )
    near_sent = jnp.concatenate([near[:half], near[half:].astype(f32) + by_over.astype(f32)], axis=0)
    over_sent = jnp.concatenate([over[:half].astype(f32) + by_near.astype(f32), over[half:]], axis=0)
    near_sent, over_sent, *last_given = together(near_sent.astype(bf16), over_sent.astype(bf16), *last_given)
    from_near = swap(near_sent, 1)
    from_over = swap(over_sent, 2)
    last_done = last(*last_given) if last else ()
    from_over, from_near, last_done = together(from_over, from_near, last_done)
    return own.astype(f32) + from_over.astype(f32) + from_near.astype(f32), first_done, last_done


def head_fields(hot_ref, table_ref, cos_ref, sin_ref):
    length = cos_ref.shape[0]
    hot = hot_ref[...].reshape(length, hot_ref.shape[-1])
    field = dot(jnp.concatenate([hot, hot], axis=1), table_ref[...].reshape(table_ref.shape[0], 3 * HEAD))
    cosine, sine = cos_ref[...], sin_ref[...]
    queries, keys, values = field[:, :HEAD], field[:, HEAD : 2 * HEAD], field[:, 2 * HEAD :]
    queries = queries * cosine + pltpu.roll(queries, HEAD // 2, 1) * sine
    keys = keys * cosine + pltpu.roll(keys, HEAD // 2, 1) * sine
    return queries.astype(bf16), keys.astype(bf16), values.astype(bf16)


def softmax_columns(keys, block, first, prefix):
    raw = dot(keys, block, LAST)
    key_pos = lax.broadcasted_iota(jnp.int32, raw.shape, 0)
    query_pos = lax.broadcasted_iota(jnp.int32, (1, raw.shape[1]), 1) + first
    raw = jnp.where(key_pos < jnp.maximum(prefix, query_pos + 1), raw, -1e30)
    top = jnp.max(raw, axis=0, keepdims=True)
    expo = jnp.exp2((raw - top) * (score_scale * LOG2_E))
    return expo, jnp.sum(expo, axis=0, keepdims=True)


def attend_kernel(prefix_ref, hot_ref, table_ref, cos_ref, sin_ref, out_ref, query_ref):
    prefix = prefix_ref[pl.program_id(0)]
    queries, keys, values = head_fields(hot_ref, table_ref, cos_ref, sin_ref)
    query_ref[...] = queries
    blocks, _, size, _ = out_ref.shape
    for b in range(blocks):
        raw = dot(query_ref[b * size : (b + 1) * size], keys, LAST)
        key_pos = lax.broadcasted_iota(jnp.int32, (1, raw.shape[1]), 1)
        query_pos = lax.broadcasted_iota(jnp.int32, (size, 1), 0) + b * size
        raw = jnp.where(key_pos < jnp.maximum(prefix, query_pos + 1), raw, -1e30)
        top = jnp.max(raw, axis=1, keepdims=True)
        expo = jnp.exp2((raw - top) * (score_scale * LOG2_E))
        total = jnp.sum(expo, axis=1, keepdims=True)
        out_ref[b, 0] = (dot(expo.astype(bf16), values) * (1.0 / total)).astype(bf16)


def attend_back_kernel(place_ref, prefix_ref, hot_ref, table_ref, cos_ref, sin_ref, grad_ref, out_ref, query_ref, key_sum, value_sum):
    prefix = prefix_ref[pl.program_id(0)]
    head = pl.program_id(1)
    queries, keys, values = head_fields(hot_ref, table_ref, cos_ref, sin_ref)
    query_ref[...] = queries
    keys_t = keys.T
    blocks, _, size, _ = grad_ref.shape
    width = out_ref.shape[-1] // 3

    def store(b, part, block):
        column = pl.multiple_of(part * width + head * HEAD, HEAD)
        out_ref[lax.bitwise_xor(place_ref[0], b), 0, :, pl.ds(column, HEAD)] = block.astype(bf16)

    def unrotated(block, b):
        rows = slice(b * size, (b + 1) * size)
        block = block * score_scale
        return block * cos_ref[rows] - pltpu.roll(block, HEAD // 2, 1) * sin_ref[rows]

    for b in range(blocks):
        block = query_ref[b * size : (b + 1) * size]
        grad = grad_ref[b, 0]
        expo, total = softmax_columns(keys, block, b * size, prefix)
        probs = expo * (1.0 / total)
        d_probs = dot(values, grad, LAST)
        inner = jnp.sum(probs * d_probs, axis=0, keepdims=True)
        d_scores = (probs * (d_probs - inner)).astype(bf16)
        key_part = dot(d_scores, block)
        value_part = dot(probs.astype(bf16), grad)
        if b == 0:
            key_sum[...] = key_part
            value_sum[...] = value_part
        else:
            key_sum[...] += key_part
            value_sum[...] += value_part
        store(b, 0, unrotated(dot(keys_t, d_scores).T, b))
    for b in range(blocks):
        rows = slice(b * size, (b + 1) * size)
        store(b, 1, unrotated(key_sum[rows], b))
        store(b, 2, value_sum[rows])


def attention_specs(groups, size, vocab, twice):
    length = groups * size
    return [
        pl.BlockSpec(memory_space=pltpu.SMEM),
        pl.BlockSpec((groups, 1, size, vocab), lambda s, h: (0, s, 0, 0)),
        pl.BlockSpec((twice, 3, HEAD), lambda s, h: (0, 0, h)),
        pl.BlockSpec((length, HEAD), lambda s, h: (0, 0)),
        pl.BlockSpec((length, HEAD), lambda s, h: (0, 0)),
    ]


def attend(prefix, hot, table, cosine, sine):
    groups, seqs, size, vocab = hot.shape
    heads = table.shape[2] // HEAD
    length = groups * size
    return pl.pallas_call(
        attend_kernel,
        grid=(seqs, heads),
        in_specs=attention_specs(groups, size, vocab, table.shape[0]),
        out_specs=pl.BlockSpec((groups, 1, size, HEAD), lambda s, h: (0, s, 0, h)),
        out_shape=jax.ShapeDtypeStruct((groups, seqs, size, heads * HEAD), bf16),
        scratch_shapes=[pltpu.VMEM((length, HEAD), bf16)],
        compiler_params=pltpu.CompilerParams(vmem_limit_bytes=48 << 20),
        cost_estimate=pl.CostEstimate(
            flops=4 * seqs * heads * length * length * HEAD,
            bytes_accessed=4 * length * heads * HEAD * seqs,
            transcendentals=seqs * heads * length * length,
        ),
    )(prefix, hot, table, cosine, sine)


def attend_back(prefix, hot, table, cosine, sine, grad):
    groups, seqs, size, vocab = hot.shape
    heads = table.shape[2] // HEAD
    length = groups * size
    return pl.pallas_call(
        attend_back_kernel,
        grid=(seqs, heads),
        in_specs=[pl.BlockSpec(memory_space=pltpu.SMEM)]
        + attention_specs(groups, size, vocab, table.shape[0])
        + [pl.BlockSpec((groups, 1, size, HEAD), lambda s, h: (0, s, 0, h))],
        out_specs=pl.BlockSpec((groups, 1, size, 3 * heads * HEAD), lambda s, h: (0, s, 0, 0)),
        out_shape=jax.ShapeDtypeStruct((groups, seqs, size, 3 * heads * HEAD), bf16),
        scratch_shapes=[
            pltpu.VMEM((length, HEAD), bf16),
            pltpu.VMEM((length, HEAD), f32),
            pltpu.VMEM((length, HEAD), f32),
        ],
        compiler_params=pltpu.CompilerParams(vmem_limit_bytes=48 << 20),
        cost_estimate=pl.CostEstimate(
            flops=10 * seqs * heads * length * length * HEAD,
            bytes_accessed=10 * length * heads * HEAD * seqs,
            transcendentals=seqs * heads * length * length,
        ),
    )(place("seq"), prefix, hot, table, cosine, sine, grad)


def on_device(
    token_ids,
    target_ids,
    prefix_lengths,
    cluster_ids,
    cluster_counts,
    embedding,
    qkv_weight,
    out_weight,
    norm1_gain,
    norm1_bias,
    gate_weight,
    up_weight,
    down_weight,
    norm2_gain,
    norm2_bias,
):
    seqs, local_len = token_ids.shape
    count = seqs * local_len
    groups = lax.axis_size("seq")
    dps = lax.axis_size("dp")
    devices = groups * dps
    seq_len = local_len * groups
    my_seq = lax.axis_index("seq")
    my_dp = lax.axis_index("dp")
    positions = my_seq * local_len + jnp.arange(local_len, dtype=jnp.int32)
    rows = qkv_weight.shape[0]
    width = embedding.shape[1]
    vocab_here = embedding.shape[0]
    vocab = vocab_here * devices
    hidden_units = gate_weight.shape[1]
    share = -(-hidden_units // (groups * LANES)) * LANES
    heads_here = HEADS // groups
    head_cols = heads_here * HEAD

    extra = jnp.concatenate(
        [norm1_gain, norm1_bias, norm2_gain, norm2_bias, token_ids.reshape(-1).astype(bf16)]
    )
    extra = jnp.pad(extra, (0, width - extra.shape[0])).reshape(1, width)
    pack = jnp.concatenate([embedding, extra], axis=0)
    chips = dps // 2
    packs = jnp.stack([pack] + [swap(pack, k) for k in range(1, groups)])
    qkv_blocks = swap_all(take_columns(qkv_weight, groups, 3, head_cols))
    packs = jnp.stack([packs] + [swap_dp(packs, 2 * j) for j in range(1, chips)])

    ff_weights = (gate_weight, up_weight, down_weight)
    ff_cols = jnp.concatenate([take_columns(weight, groups, 1, share) for weight in ff_weights], axis=2)
    ff_blocks = swap_all(ff_cols)
    out_mine, packs = together(out_weight, packs)
    packs = jnp.stack([packs, swap_dp(packs, 1)])
    qkv_cols = join_rows(qkv_blocks)
    out_blocks = jnp.stack([out_mine] + [swap_dp(out_mine, 2 * j) for j in range(1, chips)])

    owner = lax.bitwise_xor(my_dp, jnp.arange(2)[:, None] + 2 * jnp.arange(chips)[None, :])
    sender = owner[:, :, None] * groups + lax.bitwise_xor(my_seq, jnp.arange(groups))
    order = (jnp.arange(devices)[:, None] == sender.reshape(1, devices)).astype(bf16)
    packs = dot(order, packs.reshape(devices, (vocab_here + 1) * width)).reshape(devices, vocab_here + 1, width)
    embed_table = packs[:, :vocab_here].reshape(vocab, width).astype(bf16)
    extras = packs[:, vocab_here]
    norms = extras[:, : 4 * rows].reshape(devices, 4, rows)
    norms = norms.transpose(1, 0, 2).reshape(4, width)
    gain_one, bias_one, gain_two, bias_two = norms[0], norms[1], norms[2], norms[3]
    tokens_all = lax.dynamic_slice_in_dim(extras[:, 4 * rows : 4 * rows + count], my_dp * groups, groups, 0)
    tokens_all = tokens_all.astype(jnp.int32).reshape(groups, seqs, local_len)
    vocab_ids = jnp.arange(vocab, dtype=jnp.int32)
    token_hot = (token_ids.reshape(count)[:, None] == vocab_ids[None, :]).astype(bf16)

    piece = vocab // dps
    row_ids = (owner[:, :, None] * piece + jnp.arange(piece)).reshape(vocab).astype(jnp.int32)
    row_hot = (row_ids[:, None] == vocab_ids[None, :]).astype(bf16)
    all_hot = (tokens_all[..., None] == row_ids).astype(bf16)
    embed_dp = lax.dynamic_slice_in_dim(embed_table, my_dp * groups * rows, groups * rows, 1)
    qkv_part = dot(dot(row_hot, embed_dp).astype(bf16), qkv_cols)
    qkv_rows = sum_dp(qkv_part.reshape(2, chips, piece, 3 * head_cols))

    qkv_rows, out_blocks = together(qkv_rows, out_blocks)
    qkv_table, chip_rows = spread_dp(halves(qkv_rows))
    qkv_table = qkv_table.transpose(2, 0, 1, 3, 4)

    ff_cols, qkv_cols, _ = together(join_rows(ff_blocks), qkv_cols, chip_rows)
    gate_w, up_w, down_w, qkv_w = (
        lax.all_gather(cols, "dp", axis=0, tiled=True)
        for cols in (*(ff_cols[:, i * share : (i + 1) * share] for i in range(3)), qkv_cols)
    )
    qkv_table = qkv_table.reshape(2 * vocab, 3, head_cols)
    angles = rotary_angles(jnp.arange(seq_len, dtype=jnp.int32), HEAD)
    cosine, sine = jnp.cos(angles), jnp.sin(angles)
    cosine = jnp.concatenate([cosine, cosine], axis=1)
    sine = jnp.concatenate([-sine, sine], axis=1)

    context = attend(prefix_lengths, all_hot, qkv_table, cosine, sine)
    out_blocks = gather_blocks(out_blocks, context)
    out_full = join_out(out_blocks, swap_dp(out_blocks, 1))
    context = exchange(context, "seq").reshape(groups, count, head_cols)
    context = context.transpose(1, 0, 2).reshape(count, width)

    inputs = dot(token_hot, embed_table)
    hidden, norm_one_pull = jax.vjp(
        layer_norm, deep_alpha * inputs + dot(context, out_full), gain_one, bias_one
    )

    def forward(k, block):
        values = gated_gelu(dot(block, gate_w), dot(block, up_w))
        return tuple(value.astype(bf16) for value in values)

    hidden_blocks, values = gather_tokens(hidden.astype(bf16), forward)
    products, gate_slopes, up_slopes = zip(*values)
    branch = scatter_tokens(lambda k: dot(products[k], down_w, LAST))[0]
    normed, norm_two_pull = jax.vjp(layer_norm, deep_alpha * hidden + branch, gain_two, bias_two)
    activations = normed.astype(bf16)

    logits = dot(activations, embed_table, LAST)
    cluster_hot = cluster_ids[:, None] == jnp.arange(cluster_counts.shape[0], dtype=jnp.int32)[None, :]
    members = jnp.sum(jnp.where(cluster_hot, cluster_counts[None, :], 0), axis=1).astype(f32)
    counted = (positions[None, :] >= prefix_lengths[:, None]).astype(f32)
    coefs = (
        loss_scale
        * (1.0 / members)[:, None]
        / (seq_len - prefix_lengths)[:, None].astype(f32)
        * counted
    )
    logit_exp = jnp.exp(logits - jnp.max(logits, axis=-1, keepdims=True))
    logit_probs = logit_exp / jnp.sum(logit_exp, axis=-1, keepdims=True)
    target_hot = (target_ids.reshape(count)[:, None] == vocab_ids[None, :]).astype(f32)
    d_logits = (coefs.reshape(count, 1) * (logit_probs - target_hot)).astype(bf16)
    head_grad = dot(d_logits, activations, ROWS)
    d_second, d_gain_two, d_bias_two = norm_two_pull(dot(d_logits, embed_table))

    d_second, qkv_w = together(d_second, qkv_w)

    def backward(k, block):
        d_product = dot(block, down_w)
        d_gate = (d_product * gate_slopes[k].astype(f32)).astype(bf16)
        d_up = (d_product * up_slopes[k].astype(f32)).astype(bf16)
        return d_gate, d_up

    d_blocks, values = gather_tokens(d_second.astype(bf16), backward)
    d_gates, d_ups = zip(*values)

    def weight_part(*blocks):
        return dot(jnp.concatenate(blocks[:groups]), jnp.concatenate(blocks[groups:]), ROWS).astype(bf16)

    def last_parts(*blocks):
        return weight_part(*blocks[: 2 * groups]), weight_part(*blocks[2 * groups :])

    d_hidden, gate_part, (up_part, down_part) = scatter_tokens(
        lambda k: dot(d_gates[k], gate_w, LAST) + dot(d_ups[k], up_w, LAST),
        weight_part,
        last_parts,
        (*hidden_blocks, *d_gates),
        (*hidden_blocks, *d_ups, *d_blocks, *products),
    )
    d_hidden = deep_alpha * d_second + d_hidden
    gate_rows, up_rows, down_rows = (
        lax.psum_scatter(part, "dp", scatter_dimension=0, tiled=True)
        for part in (gate_part, up_part, down_part)
    )

    d_first, d_gain_one, d_bias_one = norm_one_pull(d_hidden)
    d_attention = d_first.astype(bf16)
    d_context = dot(d_attention, out_full, LAST).astype(bf16)
    d_context = d_context.reshape(count, groups, head_cols).transpose(1, 0, 2)
    d_context = exchange(d_context, "seq").reshape(groups, seqs, local_len, head_cols)

    out_part = dot(context, d_attention, ROWS).astype(bf16)
    first_low = halves(d_first)
    lookup_first = dot(token_hot, first_low[0], ROWS) + dot(token_hot, first_low[1], ROWS)
    embed_part = head_grad + (lookup_scale * deep_alpha) * lookup_first
    out_part, embed_part, d_context = together(out_part, embed_part, d_context)
    out_rows = lax.psum_scatter(out_part, "dp", scatter_dimension=0, tiled=True)

    def back(s, *before):
        grad = together(d_context[:, s : s + 1], *before)[0]
        block = attend_back(
            prefix_lengths[s : s + 1], all_hot[:, s : s + 1], qkv_table, cosine, sine, grad
        )
        return block.reshape(seq_len, 3 * head_cols)

    def own_rows(mine, *before):
        mine = together(mine, *before)[0]
        return swap_all(take_rows(mine, groups))

    gate_blocks = own_rows(gate_rows, d_context)
    d_qkv, input_blocks = [], []
    for s in range(seqs):
        block = back(s, *input_blocks[-1][0]) if s else back(s)
        part = dot(block, qkv_w, LAST).astype(bf16).reshape(groups, local_len, width)
        if s:
            block, input_blocks[-1] = together(block, input_blocks[-1])
        d_qkv.append(block)
        blocks = swap_all(part)
        input_blocks.append(([part[0]], blocks))
    up_blocks = own_rows(up_rows, d_qkv[0])
    input_grad = deep_alpha * d_first + jnp.concatenate(
        [sum(block.astype(f32) for block in blocks) for _, blocks in input_blocks]
    )

    tokens_near = jnp.stack(
        [lax.dynamic_index_in_dim(tokens_all, lax.bitwise_xor(my_seq, k), 0, False) for k in range(groups)]
    )
    near_hot = (tokens_near[..., None] == row_ids).astype(bf16)
    qkv_sums = sum(dot(near_hot[:, s].reshape(seq_len, vocab), d_qkv[s], ROWS) for s in range(seqs))
    sums_low = halves(qkv_sums)
    sums_low = jnp.stack([dot(row_hot, sums_low[0], ROWS), dot(row_hot, sums_low[1], ROWS)]).astype(bf16)
    lookup = dot(sums_low.reshape(2 * vocab, 3 * head_cols), qkv_w, LAST)
    embed_part = embed_part + lookup_scale * (lookup[:vocab] + lookup[vocab:])
    norm_part = jnp.stack([d_gain_one, d_bias_one, d_gain_two, d_bias_two])
    norm_part = norm_part.reshape(4, devices, rows).transpose(1, 0, 2).reshape(devices, 4 * rows)
    norm_part = jnp.pad(norm_part, ((0, 0), (0, width - 4 * rows))).reshape(devices, 1, width)
    small = jnp.concatenate([embed_part.reshape(devices, vocab_here, width), norm_part], axis=1)
    sums_mine = sum_dp(qkv_sums.reshape(2, chips, piece, 3 * head_cols))
    small, sums_mine, gate_blocks, up_blocks = together(small, sums_mine, gate_blocks, up_blocks)
    small = jnp.sum(exchange(small, BOTH), axis=0)
    embedding_grad = small[:vocab_here]
    norm_grads = small[vocab_here, : 4 * rows].reshape(4, rows)

    sums_all = spread(sums_mine.astype(bf16), BOTH).reshape(dps, groups, piece, 3 * head_cols)
    embed_rows = lax.dynamic_slice_in_dim(embed_table, (my_dp * groups + my_seq) * rows, rows, 1)
    qkv_grad = table_grad(sums_all, embed_rows)

    down_blocks = own_rows(down_rows, sums_mine)
    out_grad = sum(block.astype(f32) for block in own_rows(out_rows, sums_mine))
    gate_grad = join_columns(gate_blocks, hidden_units)
    up_grad = join_columns(up_blocks, hidden_units)
    down_grad = join_columns(down_blocks, hidden_units)

    return (
        activations.reshape(seqs, local_len, width),
        input_grad.reshape(seqs, local_len, width),
        embedding_grad,
        qkv_grad,
        out_grad,
        norm_grads[0],
        norm_grads[1],
        gate_grad,
        up_grad,
        down_grad,
        norm_grads[2],
        norm_grads[3],
    )


def solution(mesh):
    split = P(BOTH, None)
    line = P(BOTH)
    return jax.shard_map(
        on_device,
        mesh=mesh,
        in_specs=(
            P("dp", "seq"),
            P("dp", "seq"),
            P("dp"),
            P("dp"),
            P(),
            split,
            split,
            split,
            line,
            line,
            split,
            split,
            split,
            line,
            line,
        ),
        out_specs=(
            P("dp", "seq", None),
            P("dp", "seq", None),
            split,
            split,
            split,
            line,
            line,
            split,
            split,
            split,
            line,
            line,
        ),
        check_vma=False,
    )
```

```python
import math

import jax
import jax.numpy as jnp
from jax import lax
from jax.experimental import pallas as pl
from jax.experimental.pallas import tpu as pltpu
from jax.sharding import PartitionSpec as P

HEADS = 16
HEAD = 128
LANES = 128

deep_alpha = math.sqrt(48.0)
loss_scale = 1024.0
norm_epsilon = 1e-05
lookup_scale = 0.1
score_scale = 1.0 / math.sqrt(HEAD)
LOG2_E = math.log2(math.e)

bf16 = jnp.bfloat16
f32 = jnp.float32
BOTH = ("dp", "seq")
ROWS = (((0,), (0,)), ((), ()))
LAST = (((1,), (1,)), ((), ()))


def dot(left, right, dims=(((1,), (0,)), ((), ()))):
    return lax.dot_general(left, right, dims, preferred_element_type=f32)


def layer_norm(inputs_row, gain_row, bias_row):
    centred = inputs_row - jnp.mean(inputs_row, axis=-1, keepdims=True)
    spread_sq = jnp.mean(centred * centred, axis=-1, keepdims=True)
    return centred * lax.rsqrt(spread_sq + norm_epsilon) * gain_row + bias_row


def rotary_angles(positions, head_size):
    halves = head_size // 2
    freqs = jnp.power(10000.0, -2.0 * jnp.arange(halves, dtype=f32) / head_size)
    return positions.astype(f32)[:, None] * freqs[None, :]


def rotate(field, cosine, sine):
    halves = field.shape[-1] // 2
    first, second = field[..., :halves], field[..., halves:]
    return jnp.concatenate([first * cosine - second * sine, second * cosine + first * sine], axis=-1)


def gated_gelu(gate, up):
    root = math.sqrt(2.0 / math.pi)
    square = gate * gate
    bend = jnp.tanh(gate * (root + (root * 0.044715) * square))
    half = 0.5 + 0.5 * bend
    gelu = gate * half
    slope = half + gate * (0.5 - 0.5 * bend * bend) * (root + (3.0 * root * 0.044715) * square)
    return gelu * up, slope * up, gelu


def halves(value):
    high = lax.reduce_precision(value, 8, 7)
    return jnp.stack([high.astype(bf16), (value - high).astype(bf16)])


def together(*values):
    return lax.optimization_barrier(values)


def exchange(blocks, axes):
    return lax.all_to_all(blocks, axes, split_axis=0, concat_axis=0, tiled=True)


def spread(block, axes):
    count = lax.axis_size(axes)
    return exchange(jnp.broadcast_to(block[None], (count,) + block.shape), axes)


def swap(block, bits):
    return lax.ppermute(block, "seq", [(s, s ^ bits) for s in range(lax.axis_size("seq"))])


def swap_dp(block, bits):
    return lax.ppermute(block, "dp", [(d, d ^ bits) for d in range(lax.axis_size("dp"))])


def place(axis):
    return lax.axis_index(axis).astype(jnp.int32).reshape(1)


def take_columns(weight, groups, pieces, size):
    rows, columns = weight.shape

    def kernel(place_ref, weight_ref, out_ref):
        for g in range(groups):
            for i in range(pieces):
                first = (i * groups + g) * size
                block = weight_ref[:, first : min(first + size, columns)]
                if block.shape[1] < size:
                    rest = jnp.zeros((rows, size - block.shape[1]), block.dtype)
                    block = jnp.concatenate([block, rest], axis=1)
                out_ref[lax.bitwise_xor(place_ref[0], g), :, i * size : (i + 1) * size] = block

    return pl.pallas_call(
        kernel,
        in_specs=[pl.BlockSpec(memory_space=pltpu.SMEM), pl.BlockSpec(memory_space=pltpu.VMEM)],
        out_specs=pl.BlockSpec(memory_space=pltpu.VMEM),
        out_shape=jax.ShapeDtypeStruct((groups, rows, pieces * size), weight.dtype),
        compiler_params=pltpu.CompilerParams(vmem_limit_bytes=16 << 20),
    )(place("seq"), weight)


def swap_all(blocks):
    return [blocks[0]] + [swap(blocks[k], k) for k in range(1, blocks.shape[0])]


def join_rows(blocks):
    rows, columns = blocks[0].shape
    groups = len(blocks)

    def kernel(place_ref, *refs):
        for k in range(groups):
            first = pl.multiple_of(lax.bitwise_xor(place_ref[0], k) * rows, rows)
            refs[-1][pl.ds(first, rows), :] = refs[k][...]

    return pl.pallas_call(
        kernel,
        in_specs=[pl.BlockSpec(memory_space=pltpu.SMEM)] + [pl.BlockSpec(memory_space=pltpu.VMEM)] * groups,
        out_specs=pl.BlockSpec(memory_space=pltpu.VMEM),
        out_shape=jax.ShapeDtypeStruct((groups * rows, columns), blocks[0].dtype),
        compiler_params=pltpu.CompilerParams(vmem_limit_bytes=16 << 20),
    )(place("seq"), *blocks)


def take_rows(field, groups):
    rows, columns = field.shape[0] // groups, field.shape[1]

    def kernel(place_ref, field_ref, out_ref):
        for g in range(groups):
            out_ref[lax.bitwise_xor(place_ref[0], g)] = field_ref[g * rows : (g + 1) * rows]

    return pl.pallas_call(
        kernel,
        in_specs=[pl.BlockSpec(memory_space=pltpu.SMEM), pl.BlockSpec(memory_space=pltpu.VMEM)],
        out_specs=pl.BlockSpec(memory_space=pltpu.VMEM),
        out_shape=jax.ShapeDtypeStruct((groups, rows, columns), field.dtype),
        compiler_params=pltpu.CompilerParams(vmem_limit_bytes=16 << 20),
    )(place("seq"), field)


def take_groups(field, groups, rows):
    dps = field.shape[0] // (groups * rows)
    columns = field.shape[1]

    def kernel(place_ref, field_ref, out_ref):
        for d in range(dps):
            out_ref[0, d * rows : (d + 1) * rows] = field_ref[d, 0]

    return pl.pallas_call(
        kernel,
        grid_spec=pltpu.PrefetchScalarGridSpec(
            num_scalar_prefetch=1,
            grid=(groups,),
            in_specs=[
                pl.BlockSpec((dps, 1, rows, columns), lambda k, at: (0, lax.bitwise_xor(at[0], k), 0, 0))
            ],
            out_specs=pl.BlockSpec((1, dps * rows, columns), lambda k, at: (k, 0, 0)),
        ),
        out_shape=jax.ShapeDtypeStruct((groups, dps * rows, columns), field.dtype),
    )(place("seq"), field.reshape(dps, groups, rows, columns))


def join_columns(blocks, columns, pieces):
    rows, size = blocks[0].shape
    size //= pieces
    groups = len(blocks)

    def kernel(place_ref, *refs):
        for g in range(groups):
            source = lax.bitwise_xor(place_ref[0], g)
            for i in range(pieces):
                block = refs[0][:, i * size : (i + 1) * size]
                for k in range(1, groups):
                    block = jnp.where(source == k, refs[k][:, i * size : (i + 1) * size], block)
                first = (i * groups + g) * size
                end = min(first + size, columns)
                refs[-1][:, first:end] = block[:, : end - first].astype(f32)

    return pl.pallas_call(
        kernel,
        in_specs=[pl.BlockSpec(memory_space=pltpu.SMEM)] + [pl.BlockSpec(memory_space=pltpu.VMEM)] * groups,
        out_specs=pl.BlockSpec(memory_space=pltpu.VMEM),
        out_shape=jax.ShapeDtypeStruct((rows, columns), f32),
        compiler_params=pltpu.CompilerParams(vmem_limit_bytes=16 << 20),
    )(place("seq"), *blocks)


def join_out(mine, other):
    groups, chips, rows, width = mine.shape

    def kernel(seq_ref, dp_ref, mine_ref, other_ref, out_ref):
        chip = dp_ref[0] // 2
        for source, ref in enumerate((mine_ref, other_ref)):

            @pl.when(pl.program_id(0) == source)
            def _(ref=ref):
                for j in range(chips):
                    out_ref[lax.bitwise_xor(chip, j), 0, 0] = ref[0, j]

    last = groups - 1
    return pl.pallas_call(
        kernel,
        grid_spec=pltpu.PrefetchScalarGridSpec(
            num_scalar_prefetch=2,
            grid=(2, groups),
            in_specs=[
                pl.BlockSpec((1, chips, rows, width), lambda a, k, at, dp: (jnp.where(a == 0, k, last), 0, 0, 0)),
                pl.BlockSpec((1, chips, rows, width), lambda a, k, at, dp: (jnp.where(a == 0, 0, k), 0, 0, 0)),
            ],
            out_specs=pl.BlockSpec(
                (chips, 1, 1, rows, width),
                lambda a, k, at, dp: (
                    0,
                    lax.bitwise_xor(lax.rem(dp[0], 2), a),
                    lax.bitwise_xor(at[0], k),
                    0,
                    0,
                ),
            ),
        ),
        out_shape=jax.ShapeDtypeStruct((chips, 2, groups, rows, width), mine.dtype),
        compiler_params=pltpu.CompilerParams(vmem_limit_bytes=24 << 20),
    )(place("seq"), place("dp"), mine, other).reshape(chips * 2 * groups * rows, width)


def join_lanes(sequences):
    groups = len(sequences[0])
    rows, size = sequences[0][0].shape

    def kernel(place_ref, *refs):
        for s in range(len(sequences)):
            for k in range(groups):
                first = pl.multiple_of(lax.bitwise_xor(place_ref[0], k) * size, size)
                refs[-1][s * rows : (s + 1) * rows, pl.ds(first, size)] = refs[s * groups + k][...]

    blocks = [block for sequence in sequences for block in sequence]
    return pl.pallas_call(
        kernel,
        in_specs=[pl.BlockSpec(memory_space=pltpu.SMEM)]
        + [pl.BlockSpec(memory_space=pltpu.VMEM)] * len(blocks),
        out_specs=pl.BlockSpec(memory_space=pltpu.VMEM),
        out_shape=jax.ShapeDtypeStruct((len(sequences) * rows, groups * size), blocks[0].dtype),
        compiler_params=pltpu.CompilerParams(vmem_limit_bytes=16 << 20),
    )(place("seq"), *blocks)


def sum_dp(parts):
    kept = parts[0] + swap_dp(parts[1], 1)
    return kept[0] + sum(swap_dp(kept[j], 2 * j) for j in range(1, kept.shape[0]))


def spread_dp(block):
    blocks = jnp.stack([block] + [swap_dp(block, 2 * j) for j in range(1, lax.axis_size("dp") // 2)])
    return jnp.stack([blocks, swap_dp(blocks, 1)]), blocks


def gather_tokens(block, work, own_work):
    if lax.axis_size("seq") != 4:
        blocks = [block] + [swap(block, k) for k in range(1, lax.axis_size("seq"))]
        return blocks, [None] + [work(k, blocks[k]) for k in range(1, len(blocks))], own_work(block)
    half = block.shape[0] // 2
    near = swap(block, 1)
    over = swap(block, 2)
    own_done = own_work(block)
    near, over, own_done = together(near, over, own_done)
    far_one = swap(near[:half], 2)
    far_two = swap(over[half:], 1)
    near_work, over_work = work(1, near), work(2, over)
    far_one, far_two, near_work, over_work = together(far_one, far_two, near_work, over_work)
    far = jnp.concatenate([far_one, far_two], axis=0)
    return [block, near, over, far], [None, near_work, over_work, work(3, far)], own_done


def gather_blocks(block, held):
    if lax.axis_size("seq") != 4:
        return jnp.stack([block] + [swap(block, k) for k in range(1, lax.axis_size("seq"))]), held
    half = block.shape[0] // 2
    near, over, held = together(swap(block, 1), swap(block, 2), held)
    far = jnp.concatenate([swap(near[:half], 2), swap(over[half:], 1)], axis=0)
    return jnp.stack([block, near, over, far]), held


def scatter_tokens(part, given, first=None, last=None, first_given=(), last_given=()):
    if lax.axis_size("seq") != 4:
        total = part(given[0]).astype(f32)
        for k in range(1, lax.axis_size("seq")):
            total = total + swap(part(given[k]).astype(bf16), k).astype(f32)
        return total, first and first(*first_given), last and last(*last_given)
    far = part(given[3]).astype(bf16)
    half = far.shape[0] // 2
    far, given, *first_given = together(far, given[:3], *first_given)
    by_near = swap(far[:half], 1)
    by_over = swap(far[half:], 2)
    first_done = first(*first_given) if first else ()
    near, over, own = part(given[1]), part(given[2]), part(given[0])
    by_near, by_over, near, over, own, _ = together(by_near, by_over, near, over, own, first_done)
    near_sent = jnp.concatenate([near[:half], near[half:].astype(f32) + by_over.astype(f32)], axis=0)
    over_sent = jnp.concatenate([over[:half].astype(f32) + by_near.astype(f32), over[half:]], axis=0)
    near_sent, over_sent, *last_given = together(near_sent.astype(bf16), over_sent.astype(bf16), *last_given)
    from_near = swap(near_sent, 1)
    from_over = swap(over_sent, 2)
    last_done = last(*last_given) if last else ()
    from_over, from_near, last_done = together(from_over, from_near, last_done)
    return own.astype(f32) + from_over.astype(f32) + from_near.astype(f32), first_done, last_done


def head_fields(hot_ref, table_ref, cos_ref, sin_ref):
    length = cos_ref.shape[0]
    hot = hot_ref[...].reshape(length, hot_ref.shape[-1])
    field = dot(jnp.concatenate([hot, hot], axis=1), table_ref[...].reshape(table_ref.shape[0], 3 * HEAD))
    cosine, sine = cos_ref[...], sin_ref[...]
    queries, keys, values = field[:, :HEAD], field[:, HEAD : 2 * HEAD], field[:, 2 * HEAD :]
    queries = queries * cosine + pltpu.roll(queries, HEAD // 2, 1) * sine
    keys = keys * cosine + pltpu.roll(keys, HEAD // 2, 1) * sine
    return queries.astype(bf16), keys.astype(bf16), values.astype(bf16)


def softmax_columns(keys, block, first, prefix):
    raw = dot(keys, block, LAST)
    key_pos = lax.broadcasted_iota(jnp.int32, raw.shape, 0)
    query_pos = lax.broadcasted_iota(jnp.int32, (1, raw.shape[1]), 1) + first
    raw = jnp.where(key_pos < jnp.maximum(prefix, query_pos + 1), raw, -1e30)
    top = jnp.max(raw, axis=0, keepdims=True)
    expo = jnp.exp2((raw - top) * (score_scale * LOG2_E))
    return expo, jnp.sum(expo, axis=0, keepdims=True)


def attend_kernel(place_ref, prefix_ref, hot_ref, table_ref, cos_ref, sin_ref, out_ref, query_ref):
    prefix = prefix_ref[pl.program_id(0)]
    queries, keys, values = head_fields(hot_ref, table_ref, cos_ref, sin_ref)
    query_ref[...] = queries
    blocks, _, size, _ = out_ref.shape
    for b in range(blocks):
        raw = dot(query_ref[b * size : (b + 1) * size], keys, LAST)
        key_pos = lax.broadcasted_iota(jnp.int32, (1, raw.shape[1]), 1)
        query_pos = lax.broadcasted_iota(jnp.int32, (size, 1), 0) + b * size
        raw = jnp.where(key_pos < jnp.maximum(prefix, query_pos + 1), raw, -1e30)
        top = jnp.max(raw, axis=1, keepdims=True)
        expo = jnp.exp2((raw - top) * (score_scale * LOG2_E))
        total = jnp.sum(expo, axis=1, keepdims=True)
        out_ref[lax.bitwise_xor(place_ref[0], b), 0] = (dot(expo.astype(bf16), values) * (1.0 / total)).astype(bf16)


def attend_back_kernel(place_ref, prefix_ref, hot_ref, table_ref, cos_ref, sin_ref, grad_ref, out_ref, query_ref, key_sum, value_sum):
    prefix = prefix_ref[pl.program_id(0)]
    head = pl.program_id(1)
    queries, keys, values = head_fields(hot_ref, table_ref, cos_ref, sin_ref)
    query_ref[...] = queries
    keys_t = keys.T
    blocks, _, size, _ = grad_ref.shape
    width = out_ref.shape[-1] // 3

    def store(b, part, block):
        column = pl.multiple_of(part * width + head * HEAD, HEAD)
        out_ref[lax.bitwise_xor(place_ref[0], b), 0, :, pl.ds(column, HEAD)] = block.astype(bf16)

    def unrotated(block, b):
        rows = slice(b * size, (b + 1) * size)
        block = block * score_scale
        return block * cos_ref[rows] - pltpu.roll(block, HEAD // 2, 1) * sin_ref[rows]

    for b in range(blocks):
        block = query_ref[b * size : (b + 1) * size]
        grad = grad_ref[b, 0]
        expo, total = softmax_columns(keys, block, b * size, prefix)
        probs = expo * (1.0 / total)
        d_probs = dot(values, grad, LAST)
        inner = jnp.sum(probs * d_probs, axis=0, keepdims=True)
        d_scores = (probs * (d_probs - inner)).astype(bf16)
        key_part = dot(d_scores, block)
        value_part = dot(probs.astype(bf16), grad)
        if b == 0:
            key_sum[...] = key_part
            value_sum[...] = value_part
        else:
            key_sum[...] += key_part
            value_sum[...] += value_part
        store(b, 0, unrotated(dot(keys_t, d_scores).T, b))
    for b in range(blocks):
        rows = slice(b * size, (b + 1) * size)
        store(b, 1, unrotated(key_sum[rows], b))
        store(b, 2, value_sum[rows])


def attention_specs(groups, size, vocab, twice):
    length = groups * size
    return [
        pl.BlockSpec(memory_space=pltpu.SMEM),
        pl.BlockSpec((groups, 1, size, vocab), lambda s, h: (0, s, 0, 0)),
        pl.BlockSpec((twice, 3, HEAD), lambda s, h: (0, 0, h)),
        pl.BlockSpec((length, HEAD), lambda s, h: (0, 0)),
        pl.BlockSpec((length, HEAD), lambda s, h: (0, 0)),
    ]


def attend(prefix, hot, table, cosine, sine):
    groups, seqs, size, vocab = hot.shape
    heads = table.shape[2] // HEAD
    length = groups * size
    return pl.pallas_call(
        attend_kernel,
        grid=(seqs, heads),
        in_specs=[pl.BlockSpec(memory_space=pltpu.SMEM)]
        + attention_specs(groups, size, vocab, table.shape[0]),
        out_specs=pl.BlockSpec((groups, 1, size, HEAD), lambda s, h: (0, s, 0, h)),
        out_shape=jax.ShapeDtypeStruct((groups, seqs, size, heads * HEAD), bf16),
        scratch_shapes=[pltpu.VMEM((length, HEAD), bf16)],
        compiler_params=pltpu.CompilerParams(vmem_limit_bytes=48 << 20),
        cost_estimate=pl.CostEstimate(
            flops=4 * seqs * heads * length * length * HEAD,
            bytes_accessed=4 * length * heads * HEAD * seqs,
            transcendentals=seqs * heads * length * length,
        ),
    )(place("seq"), prefix, hot, table, cosine, sine)


def attend_back(prefix, hot, table, cosine, sine, grad):
    groups, seqs, size, vocab = hot.shape
    heads = table.shape[2] // HEAD
    length = groups * size
    return pl.pallas_call(
        attend_back_kernel,
        grid=(seqs, heads),
        in_specs=[pl.BlockSpec(memory_space=pltpu.SMEM)]
        + attention_specs(groups, size, vocab, table.shape[0])
        + [pl.BlockSpec((groups, 1, size, HEAD), lambda s, h: (0, s, 0, h))],
        out_specs=pl.BlockSpec((groups, 1, size, 3 * heads * HEAD), lambda s, h: (0, s, 0, 0)),
        out_shape=jax.ShapeDtypeStruct((groups, seqs, size, 3 * heads * HEAD), bf16),
        scratch_shapes=[
            pltpu.VMEM((length, HEAD), bf16),
            pltpu.VMEM((length, HEAD), f32),
            pltpu.VMEM((length, HEAD), f32),
        ],
        compiler_params=pltpu.CompilerParams(vmem_limit_bytes=48 << 20),
        cost_estimate=pl.CostEstimate(
            flops=10 * seqs * heads * length * length * HEAD,
            bytes_accessed=10 * length * heads * HEAD * seqs,
            transcendentals=seqs * heads * length * length,
        ),
    )(place("seq"), prefix, hot, table, cosine, sine, grad)


def on_device(
    token_ids,
    target_ids,
    prefix_lengths,
    cluster_ids,
    cluster_counts,
    embedding,
    qkv_weight,
    out_weight,
    norm1_gain,
    norm1_bias,
    gate_weight,
    up_weight,
    down_weight,
    norm2_gain,
    norm2_bias,
):
    seqs, local_len = token_ids.shape
    count = seqs * local_len
    groups = lax.axis_size("seq")
    dps = lax.axis_size("dp")
    devices = groups * dps
    seq_len = local_len * groups
    my_seq = lax.axis_index("seq")
    my_dp = lax.axis_index("dp")
    positions = my_seq * local_len + jnp.arange(local_len, dtype=jnp.int32)
    rows = qkv_weight.shape[0]
    width = embedding.shape[1]
    vocab_here = embedding.shape[0]
    vocab = vocab_here * devices
    hidden_units = gate_weight.shape[1]
    share = -(-hidden_units // (groups * LANES)) * LANES
    heads_here = HEADS // groups
    head_cols = heads_here * HEAD

    extra = jnp.concatenate(
        [norm1_gain, norm1_bias, norm2_gain, norm2_bias, token_ids.reshape(-1).astype(bf16)]
    )
    extra = jnp.pad(extra, (0, width - extra.shape[0])).reshape(1, width)
    pack = jnp.concatenate([embedding, extra], axis=0)
    chips = dps // 2
    packs = jnp.stack([pack] + [swap(pack, k) for k in range(1, groups)])
    qkv_blocks = swap_all(take_columns(qkv_weight, groups, 3, head_cols))
    packs = jnp.stack([packs] + [swap_dp(packs, 2 * j) for j in range(1, chips)])

    ff_weights = (gate_weight, up_weight, down_weight)
    ff_cols = jnp.concatenate([take_columns(weight, groups, 1, share) for weight in ff_weights], axis=2)
    ff_blocks = swap_all(ff_cols)
    out_mine, packs = together(out_weight, packs)
    packs = jnp.stack([packs, swap_dp(packs, 1)])
    qkv_cols = join_rows(qkv_blocks)
    out_blocks = jnp.stack([out_mine] + [swap_dp(out_mine, 2 * j) for j in range(1, chips)])

    owner = lax.bitwise_xor(my_dp, jnp.arange(2)[:, None] + 2 * jnp.arange(chips)[None, :])
    sender = owner[:, :, None] * groups + lax.bitwise_xor(my_seq, jnp.arange(groups))
    order = (jnp.arange(devices)[:, None] == sender.reshape(1, devices)).astype(bf16)
    packs = dot(order, packs.reshape(devices, (vocab_here + 1) * width)).reshape(devices, vocab_here + 1, width)
    embed_table = packs[:, :vocab_here].reshape(vocab, width).astype(bf16)
    extras = packs[:, vocab_here]
    norms = extras[:, : 4 * rows].reshape(devices, 4, rows)
    norms = norms.transpose(1, 0, 2).reshape(4, width)
    gain_one, bias_one, gain_two, bias_two = norms[0], norms[1], norms[2], norms[3]
    tokens_all = lax.dynamic_slice_in_dim(extras[:, 4 * rows : 4 * rows + count], my_dp * groups, groups, 0)
    tokens_all = tokens_all.astype(jnp.int32).reshape(groups, seqs, local_len)
    vocab_ids = jnp.arange(vocab, dtype=jnp.int32)
    token_hot = (token_ids.reshape(count)[:, None] == vocab_ids[None, :]).astype(bf16)

    piece = vocab // dps
    row_ids = (owner[:, :, None] * piece + jnp.arange(piece)).reshape(vocab).astype(jnp.int32)
    row_hot = (row_ids[:, None] == vocab_ids[None, :]).astype(bf16)
    all_hot = (tokens_all[..., None] == row_ids).astype(bf16)
    embed_dp = lax.dynamic_slice_in_dim(embed_table, my_dp * groups * rows, groups * rows, 1)
    embed_dp = dot(row_hot, embed_dp).astype(bf16)
    qkv_part = dot(embed_dp, qkv_cols)
    qkv_rows = sum_dp(qkv_part.reshape(2, chips, piece, 3 * head_cols))

    qkv_rows, out_blocks = together(qkv_rows, out_blocks)
    qkv_table, chip_rows = spread_dp(halves(qkv_rows))
    qkv_table = qkv_table.transpose(2, 0, 1, 3, 4)

    ff_cols, qkv_cols, _ = together(join_rows(ff_blocks), qkv_cols, chip_rows)
    gate_w, up_w, down_w, qkv_w = (
        lax.all_gather(cols, "dp", axis=0, tiled=True)
        for cols in (*(ff_cols[:, i * share : (i + 1) * share] for i in range(3)), qkv_cols)
    )
    qkv_table = qkv_table.reshape(2 * vocab, 3, head_cols)
    angles = rotary_angles(jnp.arange(seq_len, dtype=jnp.int32), HEAD)
    cosine, sine = jnp.cos(angles), jnp.sin(angles)
    cosine = jnp.concatenate([cosine, cosine], axis=1)
    sine = jnp.concatenate([-sine, sine], axis=1)

    out_blocks, qkv_table = gather_blocks(out_blocks, qkv_table)
    contexts = []
    for s in range(seqs):
        context = attend(prefix_lengths[s : s + 1], all_hot[:, s : s + 1], qkv_table, cosine, sine)
        contexts.append(swap_all(context.reshape(groups, local_len, head_cols)))
    out_blocks, context = together(out_blocks, context)
    out_other = swap_dp(out_blocks, 1)
    context = join_lanes(contexts)
    out_full = join_out(out_blocks, out_other)

    inputs = dot(token_hot, embed_table)
    hidden, norm_one_pull = jax.vjp(
        layer_norm, deep_alpha * inputs + dot(context, out_full), gain_one, bias_one
    )

    def forward(k, block):
        values = gated_gelu(dot(block, gate_w), dot(block, up_w))
        return tuple(value.astype(bf16) for value in values)

    hidden_blocks, values, own_values = gather_tokens(
        hidden.astype(bf16), forward, lambda block: forward(0, block)
    )
    products, gate_slopes, up_slopes = zip(own_values, *values[1:])
    branch = scatter_tokens(lambda product: dot(product, down_w, LAST), products)[0]
    normed, norm_two_pull = jax.vjp(layer_norm, deep_alpha * hidden + branch, gain_two, bias_two)
    activations = normed.astype(bf16)

    logits = dot(activations, embed_table, LAST)
    cluster_hot = cluster_ids[:, None] == jnp.arange(cluster_counts.shape[0], dtype=jnp.int32)[None, :]
    members = jnp.sum(jnp.where(cluster_hot, cluster_counts[None, :], 0), axis=1).astype(f32)
    counted = (positions[None, :] >= prefix_lengths[:, None]).astype(f32)
    coefs = (
        loss_scale
        * (1.0 / members)[:, None]
        / (seq_len - prefix_lengths)[:, None].astype(f32)
        * counted
    )
    logit_exp = jnp.exp(logits - jnp.max(logits, axis=-1, keepdims=True))
    logit_probs = logit_exp / jnp.sum(logit_exp, axis=-1, keepdims=True)
    target_hot = (target_ids.reshape(count)[:, None] == vocab_ids[None, :]).astype(f32)
    d_logits = (coefs.reshape(count, 1) * (logit_probs - target_hot)).astype(bf16)
    head_grad = dot(d_logits, activations, ROWS)
    d_second, d_gain_two, d_bias_two = norm_two_pull(dot(d_logits, embed_table))

    d_second, qkv_w = together(d_second, qkv_w)

    def backward(k, block):
        d_product = dot(block, down_w)
        d_gate = (d_product * gate_slopes[k].astype(f32)).astype(bf16)
        d_up = (d_product * up_slopes[k].astype(f32)).astype(bf16)
        return d_gate, d_up

    def backward_own(block):
        d_gate, d_up = backward(0, block)
        parts = [
            dot(left, right, ROWS).astype(bf16)
            for left, right in ((hidden_blocks[0], d_gate), (hidden_blocks[0], d_up), (block, products[0]))
        ]
        return d_gate, d_up, dot(d_gate, gate_w, LAST) + dot(d_up, up_w, LAST), parts

    d_blocks, values, own_values = gather_tokens(d_second.astype(bf16), backward, backward_own)
    d_gates, d_ups = zip(own_values[:2], *values[1:])
    d_hidden_own, own_parts = own_values[2:]

    def weight_part(own_part, *blocks):
        rest = dot(jnp.concatenate(blocks[: groups - 1]), jnp.concatenate(blocks[groups - 1 :]), ROWS)
        return (own_part.astype(f32) + rest).astype(bf16)

    def last_parts(*values):
        return weight_part(*values[: 2 * groups - 1]), weight_part(*values[2 * groups - 1 :])

    def hidden_part(given):
        return dot(given[0], gate_w, LAST) + dot(given[1], up_w, LAST) if len(given) > 1 else given[0]

    d_hidden, gate_part, (up_part, down_part) = scatter_tokens(
        hidden_part,
        ((d_hidden_own,), *zip(d_gates[1:], d_ups[1:])),
        weight_part,
        last_parts,
        (own_parts[0], *hidden_blocks[1:], *d_gates[1:]),
        (own_parts[1], *hidden_blocks[1:], *d_ups[1:], own_parts[2], *d_blocks[1:], *products[1:]),
    )
    d_hidden = deep_alpha * d_second + d_hidden
    gate_rows, up_rows, down_rows = (
        lax.psum_scatter(part, "dp", scatter_dimension=0, tiled=True)
        for part in (gate_part, up_part, down_part)
    )

    d_first, d_gain_one, d_bias_one = norm_one_pull(d_hidden)
    d_attention = d_first.astype(bf16)
    d_context = dot(d_attention, out_full, LAST).astype(bf16)
    d_context = d_context.reshape(count, groups, head_cols).transpose(1, 0, 2)
    d_context = exchange(d_context, "seq").reshape(groups, seqs, local_len, head_cols)

    half = width // 2
    out_left = dot(context, d_attention[:, :half], ROWS).astype(bf16)
    out_right = dot(context, d_attention[:, half:], ROWS).astype(bf16)
    first_low = halves(d_first)
    lookup_first = dot(token_hot, first_low[0], ROWS) + dot(token_hot, first_low[1], ROWS)
    embed_part = head_grad + (lookup_scale * deep_alpha) * lookup_first
    out_left = take_groups(out_left, groups, rows)
    out_left, out_right, embed_part, d_context = together(out_left, out_right, embed_part, d_context)
    out_right = lax.psum_scatter(out_right, "dp", scatter_dimension=0, tiled=True)
    out_left = swap_all(out_left)

    def back(s, *before):
        grad = together(d_context[:, s : s + 1], *before)[0]
        block = attend_back(
            prefix_lengths[s : s + 1], all_hot[:, s : s + 1], qkv_table, cosine, sine, grad
        )
        return block.reshape(seq_len, 3 * head_cols)

    def own_rows(mine, *before):
        mine = together(mine, *before)[0]
        return swap_all(take_rows(mine, groups))

    gate_blocks = own_rows(gate_rows, d_first)
    d_context, gate_blocks = together(d_context, gate_blocks)
    d_qkv, input_blocks = [], []
    for s in range(seqs):
        block = back(s, *input_blocks[-1][:1]) if s else back(s)
        if s:
            block, input_blocks[-1] = together(block, input_blocks[-1])
        part = dot(block, qkv_w, LAST).astype(bf16).reshape(groups, local_len, width)
        if s == 0:
            up_blocks = own_rows(up_rows, block)
            part, up_blocks, out_left = together(part, up_blocks, out_left)
        block, part = together(block, part)
        d_qkv.append(block)
        input_blocks.append(swap_all(part))
    out_left, _ = together(out_left, d_qkv[-1])
    out_left = sum(block.astype(f32) for block in out_left).astype(bf16)
    out_left = lax.psum_scatter(out_left, "dp", scatter_dimension=0, tiled=True)

    tokens_near = jnp.stack(
        [lax.dynamic_index_in_dim(tokens_all, lax.bitwise_xor(my_seq, k), 0, False) for k in range(groups)]
    )
    near_hot = (tokens_near[..., None] == row_ids).astype(bf16)
    qkv_sums = sum(dot(near_hot[:, s].reshape(seq_len, vocab), d_qkv[s], ROWS) for s in range(seqs))
    sums_low = halves(qkv_sums)
    sums_low = jnp.stack([dot(row_hot, sums_low[0], ROWS), dot(row_hot, sums_low[1], ROWS)]).astype(bf16)
    lookup = dot(sums_low.reshape(2 * vocab, 3 * head_cols), qkv_w, LAST)
    embed_part = embed_part + lookup_scale * (lookup[:vocab] + lookup[vocab:])
    norm_part = halves(jnp.stack([d_gain_one, d_bias_one, d_gain_two, d_bias_two]))
    norm_part = norm_part.reshape(8, devices, rows).transpose(1, 0, 2).reshape(devices, 8 * rows)
    norm_part = jnp.pad(norm_part, ((0, 0), (0, width - 8 * rows))).reshape(devices, 1, width)
    small = embed_part.astype(bf16).reshape(devices, vocab_here, width)
    small = jnp.concatenate([small, norm_part], axis=1)
    small = jnp.sum(exchange(small, BOTH).astype(f32), axis=0)
    embedding_grad = small[:vocab_here]
    norm_grads = small[vocab_here, : 8 * rows].reshape(2, 4, rows)
    norm_grads = norm_grads[0] + norm_grads[1]

    sums_mine = sum_dp(qkv_sums.reshape(2, chips, piece, 3 * head_cols))
    sums_mine, input_blocks[-1] = together(sums_mine, input_blocks[-1])
    input_grad = deep_alpha * d_first + jnp.concatenate(
        [sum(block.astype(f32) for block in blocks) for blocks in input_blocks]
    )
    sums_all = spread_dp(sums_mine.astype(bf16))[0].reshape(vocab, 3 * head_cols)
    qkv_rows = dot(embed_dp, sums_all, ROWS).astype(bf16)
    qkv_grad = join_columns(own_rows(qkv_rows), 3 * width, 3)

    down_blocks = own_rows(down_rows, sums_mine)
    gate_grad = join_columns(gate_blocks, hidden_units, 1)
    up_grad = join_columns(up_blocks, hidden_units, 1)
    out_blocks = own_rows(out_right, qkv_grad, *down_blocks)
    down_grad = join_columns(down_blocks, hidden_units, 1)
    out_right = sum(block.astype(f32) for block in out_blocks)
    out_grad = jnp.concatenate([out_left.astype(f32), out_right], axis=1)

    return (
        activations.reshape(seqs, local_len, width),
        input_grad.reshape(seqs, local_len, width),
        embedding_grad,
        qkv_grad,
        out_grad,
        norm_grads[0],
        norm_grads[1],
        gate_grad,
        up_grad,
        down_grad,
        norm_grads[2],
        norm_grads[3],
    )


def solution(mesh):
    split = P(BOTH, None)
    line = P(BOTH)
    return jax.shard_map(
        on_device,
        mesh=mesh,
        in_specs=(
            P("dp", "seq"),
            P("dp", "seq"),
            P("dp"),
            P("dp"),
            P(),
            split,
            split,
            split,
            line,
            line,
            split,
            split,
            split,
            line,
            line,
        ),
        out_specs=(
            P("dp", "seq", None),
            P("dp", "seq", None),
            split,
            split,
            split,
            line,
            line,
            split,
            split,
            split,
            line,
            line,
        ),
        check_vma=False,
    )
```

```python
import math

import jax
import jax.numpy as jnp
from jax import lax
from jax.experimental import pallas as pl
from jax.experimental.pallas import tpu as pltpu
from jax.sharding import PartitionSpec as P

HEADS = 16
HEAD = 128
LANES = 128

deep_alpha = math.sqrt(48.0)
loss_scale = 1024.0
norm_epsilon = 1e-05
lookup_scale = 0.1
score_scale = 1.0 / math.sqrt(HEAD)
LOG2_E = math.log2(math.e)

bf16 = jnp.bfloat16
f32 = jnp.float32
BOTH = ("dp", "seq")
ROWS = (((0,), (0,)), ((), ()))
LAST = (((1,), (1,)), ((), ()))


def dot(left, right, dims=(((1,), (0,)), ((), ()))):
    return lax.dot_general(left, right, dims, preferred_element_type=f32)


def layer_norm(inputs_row, gain_row, bias_row):
    centred = inputs_row - jnp.mean(inputs_row, axis=-1, keepdims=True)
    spread_sq = jnp.mean(centred * centred, axis=-1, keepdims=True)
    return centred * lax.rsqrt(spread_sq + norm_epsilon) * gain_row + bias_row


def rotary_angles(positions, head_size):
    halves = head_size // 2
    freqs = jnp.power(10000.0, -2.0 * jnp.arange(halves, dtype=f32) / head_size)
    return positions.astype(f32)[:, None] * freqs[None, :]


def rotate(field, cosine, sine):
    halves = field.shape[-1] // 2
    first, second = field[..., :halves], field[..., halves:]
    return jnp.concatenate([first * cosine - second * sine, second * cosine + first * sine], axis=-1)


def gated_gelu(gate, up):
    root = math.sqrt(2.0 / math.pi)
    square = gate * gate
    bend = jnp.tanh(gate * (root + (root * 0.044715) * square))
    half = 0.5 + 0.5 * bend
    gelu = gate * half
    slope = half + gate * (0.5 - 0.5 * bend * bend) * (root + (3.0 * root * 0.044715) * square)
    return gelu * up, slope * up, gelu


def halves(value):
    high = lax.reduce_precision(value, 8, 7)
    return jnp.stack([high.astype(bf16), (value - high).astype(bf16)])


def together(*values):
    return lax.optimization_barrier(values)


def exchange(blocks, axes):
    return lax.all_to_all(blocks, axes, split_axis=0, concat_axis=0, tiled=True)


def spread(block, axes):
    count = lax.axis_size(axes)
    return exchange(jnp.broadcast_to(block[None], (count,) + block.shape), axes)


def swap(block, bits):
    return lax.ppermute(block, "seq", [(s, s ^ bits) for s in range(lax.axis_size("seq"))])


def swap_dp(block, bits):
    return lax.ppermute(block, "dp", [(d, d ^ bits) for d in range(lax.axis_size("dp"))])


def place(axis):
    return lax.axis_index(axis).astype(jnp.int32).reshape(1)


def take_columns(weight, groups, pieces, size):
    rows, columns = weight.shape

    def kernel(place_ref, weight_ref, out_ref):
        for g in range(groups):
            for i in range(pieces):
                first = (i * groups + g) * size
                block = weight_ref[:, first : min(first + size, columns)]
                if block.shape[1] < size:
                    rest = jnp.zeros((rows, size - block.shape[1]), block.dtype)
                    block = jnp.concatenate([block, rest], axis=1)
                out_ref[lax.bitwise_xor(place_ref[0], g), :, i * size : (i + 1) * size] = block

    return pl.pallas_call(
        kernel,
        in_specs=[pl.BlockSpec(memory_space=pltpu.SMEM), pl.BlockSpec(memory_space=pltpu.VMEM)],
        out_specs=pl.BlockSpec(memory_space=pltpu.VMEM),
        out_shape=jax.ShapeDtypeStruct((groups, rows, pieces * size), weight.dtype),
        compiler_params=pltpu.CompilerParams(vmem_limit_bytes=16 << 20),
    )(place("seq"), weight)


def swap_all(blocks):
    return [blocks[0]] + [swap(blocks[k], k) for k in range(1, blocks.shape[0])]


def join_rows(blocks):
    rows, columns = blocks[0].shape
    groups = len(blocks)

    def kernel(place_ref, *refs):
        for k in range(groups):
            first = pl.multiple_of(lax.bitwise_xor(place_ref[0], k) * rows, rows)
            refs[-1][pl.ds(first, rows), :] = refs[k][...]

    return pl.pallas_call(
        kernel,
        in_specs=[pl.BlockSpec(memory_space=pltpu.SMEM)] + [pl.BlockSpec(memory_space=pltpu.VMEM)] * groups,
        out_specs=pl.BlockSpec(memory_space=pltpu.VMEM),
        out_shape=jax.ShapeDtypeStruct((groups * rows, columns), blocks[0].dtype),
        compiler_params=pltpu.CompilerParams(vmem_limit_bytes=16 << 20),
    )(place("seq"), *blocks)


def take_rows(fields, groups):
    rows = fields[0].shape[0] // groups
    columns = [field.shape[1] for field in fields]

    def kernel(place_ref, *refs):
        for g in range(groups):
            first = 0
            for field_ref, size in zip(refs, columns):
                block = field_ref[g * rows : (g + 1) * rows]
                refs[-1][lax.bitwise_xor(place_ref[0], g), :, first : first + size] = block
                first += size

    return pl.pallas_call(
        kernel,
        in_specs=[pl.BlockSpec(memory_space=pltpu.SMEM)]
        + [pl.BlockSpec(memory_space=pltpu.VMEM)] * len(fields),
        out_specs=pl.BlockSpec(memory_space=pltpu.VMEM),
        out_shape=jax.ShapeDtypeStruct((groups, rows, sum(columns)), fields[0].dtype),
        compiler_params=pltpu.CompilerParams(vmem_limit_bytes=24 << 20),
    )(place("seq"), *fields)


def join_columns(blocks, columns, pieces, fields):
    rows, size = blocks[0].shape
    size //= pieces * fields
    groups = len(blocks)

    def kernel(place_ref, *refs):
        for g in range(groups):
            source = lax.bitwise_xor(place_ref[0], g)
            for i in range(pieces * fields):
                block = refs[0][:, i * size : (i + 1) * size]
                for k in range(1, groups):
                    block = jnp.where(source == k, refs[k][:, i * size : (i + 1) * size], block)
                out_ref = refs[groups + i // pieces]
                first = (i % pieces * groups + g) * size
                end = min(first + size, columns)
                out_ref[:, first:end] = block[:, : end - first].astype(f32)

    return pl.pallas_call(
        kernel,
        in_specs=[pl.BlockSpec(memory_space=pltpu.SMEM)] + [pl.BlockSpec(memory_space=pltpu.VMEM)] * groups,
        out_specs=[pl.BlockSpec(memory_space=pltpu.VMEM)] * fields,
        out_shape=[jax.ShapeDtypeStruct((rows, columns), f32)] * fields,
        compiler_params=pltpu.CompilerParams(vmem_limit_bytes=24 << 20),
    )(place("seq"), *blocks)


def join_out(mine, other):
    groups, chips, rows, width = mine.shape

    def kernel(seq_ref, dp_ref, mine_ref, other_ref, out_ref):
        chip = dp_ref[0] // 2
        for source, ref in enumerate((mine_ref, other_ref)):

            @pl.when(pl.program_id(0) == source)
            def _(ref=ref):
                for j in range(chips):
                    out_ref[lax.bitwise_xor(chip, j), 0, 0] = ref[0, j]

    last = groups - 1
    return pl.pallas_call(
        kernel,
        grid_spec=pltpu.PrefetchScalarGridSpec(
            num_scalar_prefetch=2,
            grid=(2, groups),
            in_specs=[
                pl.BlockSpec((1, chips, rows, width), lambda a, k, at, dp: (jnp.where(a == 0, k, last), 0, 0, 0)),
                pl.BlockSpec((1, chips, rows, width), lambda a, k, at, dp: (jnp.where(a == 0, 0, k), 0, 0, 0)),
            ],
            out_specs=pl.BlockSpec(
                (chips, 1, 1, rows, width),
                lambda a, k, at, dp: (
                    0,
                    lax.bitwise_xor(lax.rem(dp[0], 2), a),
                    lax.bitwise_xor(at[0], k),
                    0,
                    0,
                ),
            ),
        ),
        out_shape=jax.ShapeDtypeStruct((chips, 2, groups, rows, width), mine.dtype),
        compiler_params=pltpu.CompilerParams(vmem_limit_bytes=24 << 20),
    )(place("seq"), place("dp"), mine, other).reshape(chips * 2 * groups * rows, width)


def join_lanes(sequences):
    groups = len(sequences[0])
    rows, size = sequences[0][0].shape

    def kernel(place_ref, *refs):
        for s in range(len(sequences)):
            for k in range(groups):
                first = pl.multiple_of(lax.bitwise_xor(place_ref[0], k) * size, size)
                refs[-1][s * rows : (s + 1) * rows, pl.ds(first, size)] = refs[s * groups + k][...]

    blocks = [block for sequence in sequences for block in sequence]
    return pl.pallas_call(
        kernel,
        in_specs=[pl.BlockSpec(memory_space=pltpu.SMEM)]
        + [pl.BlockSpec(memory_space=pltpu.VMEM)] * len(blocks),
        out_specs=pl.BlockSpec(memory_space=pltpu.VMEM),
        out_shape=jax.ShapeDtypeStruct((len(sequences) * rows, groups * size), blocks[0].dtype),
        compiler_params=pltpu.CompilerParams(vmem_limit_bytes=16 << 20),
    )(place("seq"), *blocks)


def sum_dp(parts):
    kept = parts[0] + swap_dp(parts[1], 1)
    return kept[0] + sum(swap_dp(kept[j], 2 * j) for j in range(1, kept.shape[0]))


def spread_dp(block):
    blocks = jnp.stack([block] + [swap_dp(block, 2 * j) for j in range(1, lax.axis_size("dp") // 2)])
    return jnp.stack([blocks, swap_dp(blocks, 1)]), blocks


def gather_tokens(block, work, own_work):
    if lax.axis_size("seq") != 4:
        blocks = [block] + [swap(block, k) for k in range(1, lax.axis_size("seq"))]
        return blocks, [None] + [work(k, blocks[k]) for k in range(1, len(blocks))], own_work(block)
    half = block.shape[0] // 2
    near = swap(block, 1)
    over = swap(block, 2)
    own_done = own_work(block)
    near, over, own_done = together(near, over, own_done)
    far_one = swap(near[:half], 2)
    far_two = swap(over[half:], 1)
    near_work, over_work = work(1, near), work(2, over)
    far_one, far_two, near_work, over_work = together(far_one, far_two, near_work, over_work)
    far = jnp.concatenate([far_one, far_two], axis=0)
    return [block, near, over, far], [None, near_work, over_work, work(3, far)], own_done


def gather_blocks(block, held):
    if lax.axis_size("seq") != 4:
        return jnp.stack([block] + [swap(block, k) for k in range(1, lax.axis_size("seq"))]), held
    half = block.shape[0] // 2
    near, over, held = together(swap(block, 1), swap(block, 2), held)
    far = jnp.concatenate([swap(near[:half], 2), swap(over[half:], 1)], axis=0)
    return jnp.stack([block, near, over, far]), held


def scatter_tokens(part, given, first=None, last=None, first_given=(), last_given=()):
    if lax.axis_size("seq") != 4:
        total = part(given[0]).astype(f32)
        for k in range(1, lax.axis_size("seq")):
            total = total + swap(part(given[k]).astype(bf16), k).astype(f32)
        return total, first and first(*first_given), last and last(*last_given)
    far = part(given[3]).astype(bf16)
    half = far.shape[0] // 2
    far, given, *first_given = together(far, given[:3], *first_given)
    by_near = swap(far[:half], 1)
    by_over = swap(far[half:], 2)
    first_done = first(*first_given) if first else ()
    near, over, own = part(given[1]), part(given[2]), part(given[0])
    by_near, by_over, near, over, own, _ = together(by_near, by_over, near, over, own, first_done)
    near_sent = jnp.concatenate([near[:half], near[half:].astype(f32) + by_over.astype(f32)], axis=0)
    over_sent = jnp.concatenate([over[:half].astype(f32) + by_near.astype(f32), over[half:]], axis=0)
    near_sent, over_sent, *last_given = together(near_sent.astype(bf16), over_sent.astype(bf16), *last_given)
    from_near = swap(near_sent, 1)
    from_over = swap(over_sent, 2)
    last_done = last(*last_given) if last else ()
    from_over, from_near, last_done = together(from_over, from_near, last_done)
    return own.astype(f32) + from_over.astype(f32) + from_near.astype(f32), first_done, last_done


def head_fields(hot_ref, table_ref, cos_ref, sin_ref):
    length = cos_ref.shape[0]
    hot = hot_ref[...].reshape(length, hot_ref.shape[-1])
    field = dot(jnp.concatenate([hot, hot], axis=1), table_ref[...].reshape(table_ref.shape[0], 3 * HEAD))
    cosine, sine = cos_ref[...], sin_ref[...]
    queries, keys, values = field[:, :HEAD], field[:, HEAD : 2 * HEAD], field[:, 2 * HEAD :]
    queries = queries * cosine + pltpu.roll(queries, HEAD // 2, 1) * sine
    keys = keys * cosine + pltpu.roll(keys, HEAD // 2, 1) * sine
    return queries.astype(bf16), keys.astype(bf16), values.astype(bf16)


def softmax_columns(keys, block, first, prefix):
    raw = dot(keys, block, LAST)
    key_pos = lax.broadcasted_iota(jnp.int32, raw.shape, 0)
    query_pos = lax.broadcasted_iota(jnp.int32, (1, raw.shape[1]), 1) + first
    raw = jnp.where(key_pos < jnp.maximum(prefix, query_pos + 1), raw, -1e30)
    top = jnp.max(raw, axis=0, keepdims=True)
    expo = jnp.exp2((raw - top) * (score_scale * LOG2_E))
    return expo, jnp.sum(expo, axis=0, keepdims=True)


def attend_kernel(place_ref, prefix_ref, hot_ref, table_ref, cos_ref, sin_ref, out_ref, query_ref):
    prefix = prefix_ref[pl.program_id(0)]
    queries, keys, values = head_fields(hot_ref, table_ref, cos_ref, sin_ref)
    query_ref[...] = queries
    blocks, _, size, _ = out_ref.shape
    for b in range(blocks):
        raw = dot(query_ref[b * size : (b + 1) * size], keys, LAST)
        key_pos = lax.broadcasted_iota(jnp.int32, (1, raw.shape[1]), 1)
        query_pos = lax.broadcasted_iota(jnp.int32, (size, 1), 0) + b * size
        raw = jnp.where(key_pos < jnp.maximum(prefix, query_pos + 1), raw, -1e30)
        top = jnp.max(raw, axis=1, keepdims=True)
        expo = jnp.exp2((raw - top) * (score_scale * LOG2_E))
        total = jnp.sum(expo, axis=1, keepdims=True)
        out_ref[lax.bitwise_xor(place_ref[0], b), 0] = (dot(expo.astype(bf16), values) * (1.0 / total)).astype(bf16)


def probs_kernel(prefix_ref, hot_ref, table_ref, cos_ref, sin_ref, field_ref, probs_ref):
    prefix = prefix_ref[pl.program_id(0)]
    queries, keys, values = head_fields(hot_ref, table_ref, cos_ref, sin_ref)
    field_ref[0, 0, 0], field_ref[0, 0, 1], field_ref[0, 0, 2] = queries, keys, values
    _, _, blocks, _, size = probs_ref.shape
    for b in range(blocks):
        block = field_ref[0, 0, 0, b * size : (b + 1) * size]
        expo, total = softmax_columns(keys, block, b * size, prefix)
        probs_ref[0, 0, b] = (expo * (1.0 / total)).astype(bf16)


def attend_back_kernel(place_ref, field_ref, probs_ref, cos_ref, sin_ref, grad_ref, out_ref, key_sum, value_sum):
    head = pl.program_id(0)
    keys_t = field_ref[0, 0, 1].T
    values = field_ref[0, 0, 2]
    blocks, _, size, _ = grad_ref.shape
    width = out_ref.shape[-1] // 3

    def store(b, part, block):
        column = pl.multiple_of(part * width + head * HEAD, HEAD)
        out_ref[lax.bitwise_xor(place_ref[0], b), :, pl.ds(column, HEAD)] = block.astype(bf16)

    def unrotated(block, b):
        rows = slice(b * size, (b + 1) * size)
        block = block * score_scale
        return block * cos_ref[rows] - pltpu.roll(block, HEAD // 2, 1) * sin_ref[rows]

    for b in range(blocks):
        block = field_ref[0, 0, 0, b * size : (b + 1) * size]
        grad = grad_ref[b, 0]
        probs_low = probs_ref[0, 0, b]
        probs = probs_low.astype(f32)
        d_probs = dot(values, grad, LAST)
        inner = jnp.sum(probs * d_probs, axis=0, keepdims=True)
        d_scores = (probs * (d_probs - inner)).astype(bf16)
        key_part = dot(d_scores, block)
        value_part = dot(probs_low, grad)
        if b == 0:
            key_sum[...] = key_part
            value_sum[...] = value_part
        else:
            key_sum[...] += key_part
            value_sum[...] += value_part
        store(b, 0, unrotated(dot(keys_t, d_scores).T, b))
    for b in range(blocks):
        rows = slice(b * size, (b + 1) * size)
        store(b, 1, unrotated(key_sum[rows], b))
        store(b, 2, value_sum[rows])


def attention_specs(groups, size, vocab, twice):
    length = groups * size
    return [
        pl.BlockSpec(memory_space=pltpu.SMEM),
        pl.BlockSpec((groups, 1, size, vocab), lambda s, h: (0, s, 0, 0)),
        pl.BlockSpec((twice, 3, HEAD), lambda s, h: (0, 0, h)),
        pl.BlockSpec((length, HEAD), lambda s, h: (0, 0)),
        pl.BlockSpec((length, HEAD), lambda s, h: (0, 0)),
    ]


def attend(prefix, hot, table, cosine, sine):
    groups, seqs, size, vocab = hot.shape
    heads = table.shape[2] // HEAD
    length = groups * size
    return pl.pallas_call(
        attend_kernel,
        grid=(seqs, heads),
        in_specs=[pl.BlockSpec(memory_space=pltpu.SMEM)]
        + attention_specs(groups, size, vocab, table.shape[0]),
        out_specs=pl.BlockSpec((groups, 1, size, HEAD), lambda s, h: (0, s, 0, h)),
        out_shape=jax.ShapeDtypeStruct((groups, seqs, size, heads * HEAD), bf16),
        scratch_shapes=[pltpu.VMEM((length, HEAD), bf16)],
        compiler_params=pltpu.CompilerParams(vmem_limit_bytes=48 << 20),
        cost_estimate=pl.CostEstimate(
            flops=4 * seqs * heads * length * length * HEAD,
            bytes_accessed=4 * length * heads * HEAD * seqs,
            transcendentals=seqs * heads * length * length,
        ),
    )(place("seq"), prefix, hot, table, cosine, sine)


def probabilities(prefix, hot, table, cosine, sine):
    groups, seqs, size, vocab = hot.shape
    heads = table.shape[2] // HEAD
    length = groups * size
    return pl.pallas_call(
        probs_kernel,
        grid=(seqs, heads),
        in_specs=attention_specs(groups, size, vocab, table.shape[0]),
        out_specs=[
            pl.BlockSpec((1, 1, 3, length, HEAD), lambda s, h: (s, h, 0, 0, 0)),
            pl.BlockSpec((1, 1, groups, length, size), lambda s, h: (s, h, 0, 0, 0)),
        ],
        out_shape=[
            jax.ShapeDtypeStruct((seqs, heads, 3, length, HEAD), bf16),
            jax.ShapeDtypeStruct((seqs, heads, groups, length, size), bf16),
        ],
        compiler_params=pltpu.CompilerParams(vmem_limit_bytes=48 << 20),
        cost_estimate=pl.CostEstimate(
            flops=2 * seqs * heads * length * length * HEAD,
            bytes_accessed=2 * length * length * heads * seqs,
            transcendentals=seqs * heads * length * length,
        ),
    )(prefix, hot, table, cosine, sine)


def attend_back(s, fields, probs, cosine, sine, grad):
    groups, _, size, _ = grad.shape
    heads = fields.shape[1]
    length = groups * size
    return pl.pallas_call(
        attend_back_kernel,
        grid=(heads,),
        in_specs=[
            pl.BlockSpec(memory_space=pltpu.SMEM),
            pl.BlockSpec((1, 1, 3, length, HEAD), lambda h: (s, h, 0, 0, 0)),
            pl.BlockSpec((1, 1, groups, length, size), lambda h: (s, h, 0, 0, 0)),
            pl.BlockSpec((length, HEAD), lambda h: (0, 0)),
            pl.BlockSpec((length, HEAD), lambda h: (0, 0)),
            pl.BlockSpec((groups, 1, size, HEAD), lambda h: (0, s, 0, h)),
        ],
        out_specs=pl.BlockSpec((groups, size, 3 * heads * HEAD), lambda h: (0, 0, 0)),
        out_shape=jax.ShapeDtypeStruct((groups, size, 3 * heads * HEAD), bf16),
        scratch_shapes=[pltpu.VMEM((length, HEAD), f32), pltpu.VMEM((length, HEAD), f32)],
        compiler_params=pltpu.CompilerParams(vmem_limit_bytes=48 << 20),
        cost_estimate=pl.CostEstimate(
            flops=8 * heads * length * length * HEAD,
            bytes_accessed=2 * length * length * heads,
            transcendentals=0,
        ),
    )(place("seq"), fields, probs, cosine, sine, grad)


def on_device(
    token_ids,
    target_ids,
    prefix_lengths,
    cluster_ids,
    cluster_counts,
    embedding,
    qkv_weight,
    out_weight,
    norm1_gain,
    norm1_bias,
    gate_weight,
    up_weight,
    down_weight,
    norm2_gain,
    norm2_bias,
):
    seqs, local_len = token_ids.shape
    count = seqs * local_len
    groups = lax.axis_size("seq")
    dps = lax.axis_size("dp")
    devices = groups * dps
    seq_len = local_len * groups
    my_seq = lax.axis_index("seq")
    my_dp = lax.axis_index("dp")
    positions = my_seq * local_len + jnp.arange(local_len, dtype=jnp.int32)
    rows = qkv_weight.shape[0]
    width = embedding.shape[1]
    vocab_here = embedding.shape[0]
    vocab = vocab_here * devices
    hidden_units = gate_weight.shape[1]
    share = -(-hidden_units // (groups * LANES)) * LANES
    heads_here = HEADS // groups
    head_cols = heads_here * HEAD

    extra = jnp.concatenate(
        [norm1_gain, norm1_bias, norm2_gain, norm2_bias, token_ids.reshape(-1).astype(bf16)]
    )
    extra = jnp.pad(extra, (0, width - extra.shape[0])).reshape(1, width)
    pack = jnp.concatenate([embedding, extra], axis=0)
    chips = dps // 2
    packs = jnp.stack([pack] + [swap(pack, k) for k in range(1, groups)])
    qkv_blocks = swap_all(take_columns(qkv_weight, groups, 3, head_cols))
    packs = jnp.stack([packs] + [swap_dp(packs, 2 * j) for j in range(1, chips)])

    ff_weights = (gate_weight, up_weight, down_weight)
    ff_cols = jnp.concatenate([take_columns(weight, groups, 1, share) for weight in ff_weights], axis=2)
    ff_blocks = swap_all(ff_cols)
    out_mine, packs = together(out_weight, packs)
    packs = jnp.stack([packs, swap_dp(packs, 1)])
    qkv_cols = join_rows(qkv_blocks)
    out_blocks = jnp.stack([out_mine] + [swap_dp(out_mine, 2 * j) for j in range(1, chips)])

    owner = lax.bitwise_xor(my_dp, jnp.arange(2)[:, None] + 2 * jnp.arange(chips)[None, :])
    sender = owner[:, :, None] * groups + lax.bitwise_xor(my_seq, jnp.arange(groups))
    order = (jnp.arange(devices)[:, None] == sender.reshape(1, devices)).astype(bf16)
    packs = dot(order, packs.reshape(devices, (vocab_here + 1) * width)).reshape(devices, vocab_here + 1, width)
    embed_table = packs[:, :vocab_here].reshape(vocab, width).astype(bf16)
    extras = packs[:, vocab_here]
    norms = extras[:, : 4 * rows].reshape(devices, 4, rows)
    norms = norms.transpose(1, 0, 2).reshape(4, width)
    gain_one, bias_one, gain_two, bias_two = norms[0], norms[1], norms[2], norms[3]
    tokens_all = lax.dynamic_slice_in_dim(extras[:, 4 * rows : 4 * rows + count], my_dp * groups, groups, 0)
    tokens_all = tokens_all.astype(jnp.int32).reshape(groups, seqs, local_len)
    vocab_ids = jnp.arange(vocab, dtype=jnp.int32)
    token_hot = (token_ids.reshape(count)[:, None] == vocab_ids[None, :]).astype(bf16)

    piece = vocab // dps
    row_ids = (owner[:, :, None] * piece + jnp.arange(piece)).reshape(vocab).astype(jnp.int32)
    row_hot = (row_ids[:, None] == vocab_ids[None, :]).astype(bf16)
    all_hot = (tokens_all[..., None] == row_ids).astype(bf16)
    embed_dp = lax.dynamic_slice_in_dim(embed_table, my_dp * groups * rows, groups * rows, 1)
    embed_dp = dot(row_hot, embed_dp).astype(bf16)
    qkv_part = dot(embed_dp, qkv_cols)
    qkv_rows = sum_dp(qkv_part.reshape(2, chips, piece, 3 * head_cols))

    qkv_rows, out_blocks = together(qkv_rows, out_blocks)
    qkv_table, chip_rows = spread_dp(halves(qkv_rows))
    qkv_table = qkv_table.transpose(2, 0, 1, 3, 4)

    ff_cols, qkv_cols, _ = together(join_rows(ff_blocks), qkv_cols, chip_rows)
    gate_w, up_w, down_w, qkv_w = (
        lax.all_gather(cols, "dp", axis=0, tiled=True)
        for cols in (*(ff_cols[:, i * share : (i + 1) * share] for i in range(3)), qkv_cols)
    )
    qkv_table = qkv_table.reshape(2 * vocab, 3, head_cols)
    angles = rotary_angles(jnp.arange(seq_len, dtype=jnp.int32), HEAD)
    cosine, sine = jnp.cos(angles), jnp.sin(angles)
    cosine = jnp.concatenate([cosine, cosine], axis=1)
    sine = jnp.concatenate([-sine, sine], axis=1)

    out_blocks, qkv_table = gather_blocks(out_blocks, qkv_table)
    contexts = []
    for s in range(seqs):
        context = attend(prefix_lengths[s : s + 1], all_hot[:, s : s + 1], qkv_table, cosine, sine)
        contexts.append(swap_all(context.reshape(groups, local_len, head_cols)))
    out_blocks, context = together(out_blocks, context)
    out_other = swap_dp(out_blocks, 1)
    context = join_lanes(contexts)
    out_full = join_out(out_blocks, out_other)

    inputs = dot(token_hot, embed_table)
    hidden, norm_one_pull = jax.vjp(
        layer_norm, deep_alpha * inputs + dot(context, out_full), gain_one, bias_one
    )

    def forward(k, block):
        values = gated_gelu(dot(block, gate_w), dot(block, up_w))
        return tuple(value.astype(bf16) for value in values)

    hidden_blocks, values, own_values = gather_tokens(
        hidden.astype(bf16), forward, lambda block: forward(0, block)
    )
    products, gate_slopes, up_slopes = zip(own_values, *values[1:])
    branch, _, (fields, probs) = scatter_tokens(
        lambda product: dot(product, down_w, LAST),
        products,
        None,
        lambda table: probabilities(prefix_lengths, all_hot, table, cosine, sine),
        (),
        (qkv_table,),
    )
    normed, norm_two_pull = jax.vjp(layer_norm, deep_alpha * hidden + branch, gain_two, bias_two)
    activations = normed.astype(bf16)

    logits = dot(activations, embed_table, LAST)
    cluster_hot = cluster_ids[:, None] == jnp.arange(cluster_counts.shape[0], dtype=jnp.int32)[None, :]
    members = jnp.sum(jnp.where(cluster_hot, cluster_counts[None, :], 0), axis=1).astype(f32)
    counted = (positions[None, :] >= prefix_lengths[:, None]).astype(f32)
    coefs = (
        loss_scale
        * (1.0 / members)[:, None]
        / (seq_len - prefix_lengths)[:, None].astype(f32)
        * counted
    )
    logit_exp = jnp.exp(logits - jnp.max(logits, axis=-1, keepdims=True))
    logit_probs = logit_exp / jnp.sum(logit_exp, axis=-1, keepdims=True)
    target_hot = (target_ids.reshape(count)[:, None] == vocab_ids[None, :]).astype(f32)
    d_logits = (coefs.reshape(count, 1) * (logit_probs - target_hot)).astype(bf16)
    head_grad = dot(d_logits, activations, ROWS)
    d_second, d_gain_two, d_bias_two = norm_two_pull(dot(d_logits, embed_table))

    d_second, qkv_w = together(d_second, qkv_w)

    def backward(k, block):
        d_product = dot(block, down_w)
        d_gate = (d_product * gate_slopes[k].astype(f32)).astype(bf16)
        d_up = (d_product * up_slopes[k].astype(f32)).astype(bf16)
        return d_gate, d_up

    def backward_own(block):
        d_gate, d_up = backward(0, block)
        parts = [
            dot(left, right, ROWS).astype(bf16)
            for left, right in ((hidden_blocks[0], d_gate), (hidden_blocks[0], d_up), (block, products[0]))
        ]
        return d_gate, d_up, dot(d_gate, gate_w, LAST) + dot(d_up, up_w, LAST), parts

    d_blocks, values, own_values = gather_tokens(d_second.astype(bf16), backward, backward_own)
    d_gates, d_ups = zip(own_values[:2], *values[1:])
    d_hidden_own, own_parts = own_values[2:]

    def weight_part(own_part, *blocks):
        rest = dot(jnp.concatenate(blocks[: groups - 1]), jnp.concatenate(blocks[groups - 1 :]), ROWS)
        return (own_part.astype(f32) + rest).astype(bf16)

    def last_parts(*values):
        return weight_part(*values[: 2 * groups - 1]), weight_part(*values[2 * groups - 1 :])

    def hidden_part(given):
        return dot(given[0], gate_w, LAST) + dot(given[1], up_w, LAST) if len(given) > 1 else given[0]

    d_hidden, gate_part, (up_part, down_part) = scatter_tokens(
        hidden_part,
        ((d_hidden_own,), *zip(d_gates[1:], d_ups[1:])),
        weight_part,
        last_parts,
        (own_parts[0], *hidden_blocks[1:], *d_gates[1:]),
        (own_parts[1], *hidden_blocks[1:], *d_ups[1:], own_parts[2], *d_blocks[1:], *products[1:]),
    )
    d_hidden = deep_alpha * d_second + d_hidden
    gate_rows, up_rows, down_rows = (
        lax.psum_scatter(part, "dp", scatter_dimension=0, tiled=True)
        for part in (gate_part, up_part, down_part)
    )

    d_first, d_gain_one, d_bias_one = norm_one_pull(d_hidden)
    d_attention = d_first.astype(bf16)
    d_context = dot(d_attention, out_full, LAST).astype(bf16)
    d_context = d_context.reshape(count, groups, head_cols).transpose(1, 0, 2)
    d_context = exchange(d_context, "seq").reshape(groups, seqs, local_len, head_cols)

    out_part = dot(context, d_attention, ROWS).astype(bf16)
    first_low = halves(d_first)
    lookup_first = dot(token_hot, first_low[0], ROWS) + dot(token_hot, first_low[1], ROWS)
    embed_part = head_grad + (lookup_scale * deep_alpha) * lookup_first
    d_context, out_part = together(d_context, out_part)
    out_rows = lax.psum_scatter(out_part, "dp", scatter_dimension=0, tiled=True)

    def own_rows(fields, *before):
        fields = together(fields, *before)[0]
        return swap_all(take_rows(fields, groups))

    d_qkv, input_blocks = [], []
    for s in range(seqs):
        grad = together(d_context, *input_blocks[-1][:1])[0] if s else d_context
        block = attend_back(s, fields, probs, cosine, sine, grad).reshape(seq_len, 3 * head_cols)
        part = dot(block, qkv_w, LAST).astype(bf16).reshape(groups, local_len, width)
        if s:
            part, input_blocks[-1] = together(part, input_blocks[-1])
        block, part = together(block, part)
        d_qkv.append(block)
        input_blocks.append(swap_all(part))

    tokens_near = jnp.stack(
        [lax.dynamic_index_in_dim(tokens_all, lax.bitwise_xor(my_seq, k), 0, False) for k in range(groups)]
    )
    near_hot = (tokens_near[..., None] == row_ids).astype(bf16)
    qkv_sums = sum(dot(near_hot[:, s].reshape(seq_len, vocab), d_qkv[s], ROWS) for s in range(seqs))
    sums_low = halves(qkv_sums)
    sums_low = jnp.stack([dot(row_hot, sums_low[0], ROWS), dot(row_hot, sums_low[1], ROWS)]).astype(bf16)
    lookup = dot(sums_low.reshape(2 * vocab, 3 * head_cols), qkv_w, LAST)
    embed_part = embed_part + lookup_scale * (lookup[:vocab] + lookup[vocab:])
    norm_part = halves(jnp.stack([d_gain_one, d_bias_one, d_gain_two, d_bias_two]))
    norm_part = norm_part.reshape(8, devices, rows).transpose(1, 0, 2).reshape(devices, 8 * rows)
    norm_part = jnp.pad(norm_part, ((0, 0), (0, width - 8 * rows))).reshape(devices, 1, width)
    small = embed_part.astype(bf16).reshape(devices, vocab_here, width)
    small = jnp.concatenate([small, norm_part], axis=1)
    small = jnp.sum(exchange(small, BOTH).astype(f32), axis=0)
    embedding_grad = small[:vocab_here]
    norm_grads = small[vocab_here, : 8 * rows].reshape(2, 4, rows)
    norm_grads = norm_grads[0] + norm_grads[1]

    sums_mine = sum_dp(qkv_sums.reshape(2, chips, piece, 3 * head_cols))
    ff_blocks = own_rows([gate_rows, up_rows, down_rows], qkv_sums)
    sums_mine, input_blocks[-1], ff_blocks = together(sums_mine, input_blocks[-1], ff_blocks)
    input_grad = deep_alpha * d_first + jnp.concatenate(
        [sum(block.astype(f32) for block in blocks) for blocks in input_blocks]
    )
    sums_all = spread_dp(sums_mine.astype(bf16))[0].reshape(vocab, 3 * head_cols)
    qkv_rows = dot(embed_dp, sums_all, ROWS).astype(bf16)
    (qkv_grad,) = join_columns(own_rows([qkv_rows]), 3 * width, 3, 1)

    gate_grad, up_grad, down_grad = join_columns(ff_blocks, hidden_units, 1, 3)
    out_grad = sum(block.astype(f32) for block in own_rows([out_rows], sums_mine))

    return (
        activations.reshape(seqs, local_len, width),
        input_grad.reshape(seqs, local_len, width),
        embedding_grad,
        qkv_grad,
        out_grad,
        norm_grads[0],
        norm_grads[1],
        gate_grad,
        up_grad,
        down_grad,
        norm_grads[2],
        norm_grads[3],
    )


def solution(mesh):
    split = P(BOTH, None)
    line = P(BOTH)
    return jax.shard_map(
        on_device,
        mesh=mesh,
        in_specs=(
            P("dp", "seq"),
            P("dp", "seq"),
            P("dp"),
            P("dp"),
            P(),
            split,
            split,
            split,
            line,
            line,
            split,
            split,
            split,
            line,
            line,
        ),
        out_specs=(
            P("dp", "seq", None),
            P("dp", "seq", None),
            split,
            split,
            split,
            line,
            line,
            split,
            split,
            split,
            line,
            line,
        ),
        check_vma=False,
    )
```

```python
import math

import jax
import jax.numpy as jnp
from jax import lax
from jax.experimental import pallas as pl
from jax.experimental.pallas import tpu as pltpu
from jax.sharding import PartitionSpec as P

HEADS = 16
HEAD = 128
LANES = 128

deep_alpha = math.sqrt(48.0)
loss_scale = 1024.0
norm_epsilon = 1e-05
lookup_scale = 0.1
score_scale = 1.0 / math.sqrt(HEAD)
LOG2_E = math.log2(math.e)

bf16 = jnp.bfloat16
f32 = jnp.float32
BOTH = ("dp", "seq")
ROWS = (((0,), (0,)), ((), ()))
LAST = (((1,), (1,)), ((), ()))


def dot(left, right, dims=(((1,), (0,)), ((), ()))):
    return lax.dot_general(left, right, dims, preferred_element_type=f32)


def layer_norm(inputs_row, gain_row, bias_row):
    centred = inputs_row - jnp.mean(inputs_row, axis=-1, keepdims=True)
    spread_sq = jnp.mean(centred * centred, axis=-1, keepdims=True)
    return centred * lax.rsqrt(spread_sq + norm_epsilon) * gain_row + bias_row


def rotary_angles(positions, head_size):
    halves = head_size // 2
    freqs = jnp.power(10000.0, -2.0 * jnp.arange(halves, dtype=f32) / head_size)
    return positions.astype(f32)[:, None] * freqs[None, :]


def rotate(field, cosine, sine):
    halves = field.shape[-1] // 2
    first, second = field[..., :halves], field[..., halves:]
    return jnp.concatenate([first * cosine - second * sine, second * cosine + first * sine], axis=-1)


def gated_gelu(gate, up):
    root = math.sqrt(2.0 / math.pi)
    square = gate * gate
    bend = jnp.tanh(gate * (root + (root * 0.044715) * square))
    half = 0.5 + 0.5 * bend
    gelu = gate * half
    slope = half + gate * (0.5 - 0.5 * bend * bend) * (root + (3.0 * root * 0.044715) * square)
    return gelu * up, slope * up, gelu


def halves(value):
    high = lax.reduce_precision(value, 8, 7)
    return jnp.stack([high.astype(bf16), (value - high).astype(bf16)])


def together(*values):
    return lax.optimization_barrier(values)


def exchange(blocks, axes):
    return lax.all_to_all(blocks, axes, split_axis=0, concat_axis=0, tiled=True)


def spread(block, axes):
    count = lax.axis_size(axes)
    return exchange(jnp.broadcast_to(block[None], (count,) + block.shape), axes)


def swap(block, bits):
    return lax.ppermute(block, "seq", [(s, s ^ bits) for s in range(lax.axis_size("seq"))])


def swap_dp(block, bits):
    return lax.ppermute(block, "dp", [(d, d ^ bits) for d in range(lax.axis_size("dp"))])


def place(axis):
    return lax.axis_index(axis).astype(jnp.int32).reshape(1)


def take_columns(weight, groups, pieces, size):
    rows, columns = weight.shape

    def kernel(place_ref, weight_ref, out_ref):
        for g in range(groups):
            for i in range(pieces):
                first = (i * groups + g) * size
                block = weight_ref[:, first : min(first + size, columns)]
                if block.shape[1] < size:
                    rest = jnp.zeros((rows, size - block.shape[1]), block.dtype)
                    block = jnp.concatenate([block, rest], axis=1)
                out_ref[lax.bitwise_xor(place_ref[0], g), :, i * size : (i + 1) * size] = block

    return pl.pallas_call(
        kernel,
        in_specs=[pl.BlockSpec(memory_space=pltpu.SMEM), pl.BlockSpec(memory_space=pltpu.VMEM)],
        out_specs=pl.BlockSpec(memory_space=pltpu.VMEM),
        out_shape=jax.ShapeDtypeStruct((groups, rows, pieces * size), weight.dtype),
        compiler_params=pltpu.CompilerParams(vmem_limit_bytes=16 << 20),
    )(place("seq"), weight)


def swap_all(blocks):
    return [blocks[0]] + [swap(blocks[k], k) for k in range(1, blocks.shape[0])]


def join_rows(blocks):
    rows, columns = blocks[0].shape
    groups = len(blocks)

    def kernel(place_ref, *refs):
        for k in range(groups):
            first = pl.multiple_of(lax.bitwise_xor(place_ref[0], k) * rows, rows)
            refs[-1][pl.ds(first, rows), :] = refs[k][...]

    return pl.pallas_call(
        kernel,
        in_specs=[pl.BlockSpec(memory_space=pltpu.SMEM)] + [pl.BlockSpec(memory_space=pltpu.VMEM)] * groups,
        out_specs=pl.BlockSpec(memory_space=pltpu.VMEM),
        out_shape=jax.ShapeDtypeStruct((groups * rows, columns), blocks[0].dtype),
        compiler_params=pltpu.CompilerParams(vmem_limit_bytes=16 << 20),
    )(place("seq"), *blocks)


def take_rows(fields, groups):
    rows = fields[0].shape[0] // groups
    columns = [field.shape[1] for field in fields]

    def kernel(place_ref, *refs):
        for g in range(groups):
            first = 0
            for field_ref, size in zip(refs, columns):
                block = field_ref[g * rows : (g + 1) * rows]
                refs[-1][lax.bitwise_xor(place_ref[0], g), :, first : first + size] = block
                first += size

    return pl.pallas_call(
        kernel,
        in_specs=[pl.BlockSpec(memory_space=pltpu.SMEM)]
        + [pl.BlockSpec(memory_space=pltpu.VMEM)] * len(fields),
        out_specs=pl.BlockSpec(memory_space=pltpu.VMEM),
        out_shape=jax.ShapeDtypeStruct((groups, rows, sum(columns)), fields[0].dtype),
        compiler_params=pltpu.CompilerParams(vmem_limit_bytes=24 << 20),
    )(place("seq"), *fields)


def join_columns(blocks, columns, pieces, fields):
    rows, size = blocks[0].shape
    size //= pieces * fields
    groups = len(blocks)

    def kernel(place_ref, *refs):
        for g in range(groups):
            source = lax.bitwise_xor(place_ref[0], g)
            for i in range(pieces * fields):
                block = refs[0][:, i * size : (i + 1) * size]
                for k in range(1, groups):
                    block = jnp.where(source == k, refs[k][:, i * size : (i + 1) * size], block)
                out_ref = refs[groups + i // pieces]
                first = (i % pieces * groups + g) * size
                end = min(first + size, columns)
                out_ref[:, first:end] = block[:, : end - first].astype(f32)

    return pl.pallas_call(
        kernel,
        in_specs=[pl.BlockSpec(memory_space=pltpu.SMEM)] + [pl.BlockSpec(memory_space=pltpu.VMEM)] * groups,
        out_specs=[pl.BlockSpec(memory_space=pltpu.VMEM)] * fields,
        out_shape=[jax.ShapeDtypeStruct((rows, columns), f32)] * fields,
        compiler_params=pltpu.CompilerParams(vmem_limit_bytes=24 << 20),
    )(place("seq"), *blocks)


def join_out(mine, other):
    groups, chips, rows, width = mine.shape

    def kernel(seq_ref, dp_ref, mine_ref, other_ref, out_ref):
        chip = dp_ref[0] // 2
        for source, ref in enumerate((mine_ref, other_ref)):

            @pl.when(pl.program_id(0) == source)
            def _(ref=ref):
                for j in range(chips):
                    out_ref[lax.bitwise_xor(chip, j), 0, 0] = ref[0, j]

    last = groups - 1
    return pl.pallas_call(
        kernel,
        grid_spec=pltpu.PrefetchScalarGridSpec(
            num_scalar_prefetch=2,
            grid=(2, groups),
            in_specs=[
                pl.BlockSpec((1, chips, rows, width), lambda a, k, at, dp: (jnp.where(a == 0, k, last), 0, 0, 0)),
                pl.BlockSpec((1, chips, rows, width), lambda a, k, at, dp: (jnp.where(a == 0, 0, k), 0, 0, 0)),
            ],
            out_specs=pl.BlockSpec(
                (chips, 1, 1, rows, width),
                lambda a, k, at, dp: (
                    0,
                    lax.bitwise_xor(lax.rem(dp[0], 2), a),
                    lax.bitwise_xor(at[0], k),
                    0,
                    0,
                ),
            ),
        ),
        out_shape=jax.ShapeDtypeStruct((chips, 2, groups, rows, width), mine.dtype),
        compiler_params=pltpu.CompilerParams(vmem_limit_bytes=24 << 20),
    )(place("seq"), place("dp"), mine, other).reshape(chips * 2 * groups * rows, width)


def join_lanes(sequences):
    groups = len(sequences[0])
    rows, size = sequences[0][0].shape

    def kernel(place_ref, *refs):
        for s in range(len(sequences)):
            for k in range(groups):
                first = pl.multiple_of(lax.bitwise_xor(place_ref[0], k) * size, size)
                refs[-1][s * rows : (s + 1) * rows, pl.ds(first, size)] = refs[s * groups + k][...]

    blocks = [block for sequence in sequences for block in sequence]
    return pl.pallas_call(
        kernel,
        in_specs=[pl.BlockSpec(memory_space=pltpu.SMEM)]
        + [pl.BlockSpec(memory_space=pltpu.VMEM)] * len(blocks),
        out_specs=pl.BlockSpec(memory_space=pltpu.VMEM),
        out_shape=jax.ShapeDtypeStruct((len(sequences) * rows, groups * size), blocks[0].dtype),
        compiler_params=pltpu.CompilerParams(vmem_limit_bytes=16 << 20),
    )(place("seq"), *blocks)


def sum_dp(parts, kind):
    kept = parts[0] + swap_dp(parts[1].astype(kind), 1).astype(f32)
    sent = kept.astype(kind)
    return kept[0] + sum(swap_dp(sent[j], 2 * j).astype(f32) for j in range(1, kept.shape[0]))


def spread_dp(block):
    blocks = jnp.stack([block] + [swap_dp(block, 2 * j) for j in range(1, lax.axis_size("dp") // 2)])
    return jnp.stack([blocks, swap_dp(blocks, 1)]), blocks


def gather_tokens(block, work, own_work):
    if lax.axis_size("seq") != 4:
        blocks = [block] + [swap(block, k) for k in range(1, lax.axis_size("seq"))]
        return blocks, [None] + [work(k, blocks[k]) for k in range(1, len(blocks))], own_work(block)
    half = block.shape[0] // 2
    near = swap(block, 1)
    over = swap(block, 2)
    own_done = own_work(block)
    near, over, own_done = together(near, over, own_done)
    far_one = swap(near[:half], 2)
    far_two = swap(over[half:], 1)
    near_work, over_work = work(1, near), work(2, over)
    far_one, far_two, near_work, over_work = together(far_one, far_two, near_work, over_work)
    far = jnp.concatenate([far_one, far_two], axis=0)
    return [block, near, over, far], [None, near_work, over_work, work(3, far)], own_done


def gather_blocks(block, held):
    if lax.axis_size("seq") != 4:
        return jnp.stack([block] + [swap(block, k) for k in range(1, lax.axis_size("seq"))]), held
    half = block.shape[0] // 2
    near, over, held = together(swap(block, 1), swap(block, 2), held)
    far = jnp.concatenate([swap(near[:half], 2), swap(over[half:], 1)], axis=0)
    return jnp.stack([block, near, over, far]), held


def scatter_tokens(part, given, first=None, last=None, first_given=(), last_given=()):
    if lax.axis_size("seq") != 4:
        total = part(given[0]).astype(f32)
        for k in range(1, lax.axis_size("seq")):
            total = total + swap(part(given[k]).astype(bf16), k).astype(f32)
        return total, first and first(*first_given), last and last(*last_given)
    far = part(given[3]).astype(bf16)
    half = far.shape[0] // 2
    far, given, *first_given = together(far, given[:3], *first_given)
    by_near = swap(far[:half], 1)
    by_over = swap(far[half:], 2)
    first_done = first(*first_given) if first else ()
    near, over, own = part(given[1]), part(given[2]), part(given[0])
    by_near, by_over, near, over, own, _ = together(by_near, by_over, near, over, own, first_done)
    near_sent = jnp.concatenate([near[:half], near[half:].astype(f32) + by_over.astype(f32)], axis=0)
    over_sent = jnp.concatenate([over[:half].astype(f32) + by_near.astype(f32), over[half:]], axis=0)
    near_sent, over_sent, *last_given = together(near_sent.astype(bf16), over_sent.astype(bf16), *last_given)
    from_near = swap(near_sent, 1)
    from_over = swap(over_sent, 2)
    last_done = last(*last_given) if last else ()
    from_over, from_near, last_done = together(from_over, from_near, last_done)
    return own.astype(f32) + from_over.astype(f32) + from_near.astype(f32), first_done, last_done


def head_fields(hot_ref, table_ref, cos_ref, sin_ref):
    length = cos_ref.shape[0]
    hot = hot_ref[...].reshape(length, hot_ref.shape[-1])
    field = dot(jnp.concatenate([hot, hot], axis=1), table_ref[...].reshape(table_ref.shape[0], 3 * HEAD))
    cosine, sine = cos_ref[...], sin_ref[...]
    queries, keys, values = field[:, :HEAD], field[:, HEAD : 2 * HEAD], field[:, 2 * HEAD :]
    queries = queries * cosine + pltpu.roll(queries, HEAD // 2, 1) * sine
    keys = keys * cosine + pltpu.roll(keys, HEAD // 2, 1) * sine
    return queries.astype(bf16), keys.astype(bf16), values.astype(bf16)


def softmax_columns(keys, block, first, prefix):
    raw = dot(keys, block, LAST)
    key_pos = lax.broadcasted_iota(jnp.int32, raw.shape, 0)
    query_pos = lax.broadcasted_iota(jnp.int32, (1, raw.shape[1]), 1) + first
    raw = jnp.where(key_pos < jnp.maximum(prefix, query_pos + 1), raw, -1e30)
    top = jnp.max(raw, axis=0, keepdims=True)
    expo = jnp.exp2((raw - top) * (score_scale * LOG2_E))
    return expo, jnp.sum(expo, axis=0, keepdims=True)


def attend_kernel(place_ref, prefix_ref, hot_ref, table_ref, cos_ref, sin_ref, out_ref, query_ref):
    prefix = prefix_ref[pl.program_id(0)]
    queries, keys, values = head_fields(hot_ref, table_ref, cos_ref, sin_ref)
    query_ref[...] = queries
    blocks, _, size, _ = out_ref.shape
    for b in range(blocks):
        raw = dot(query_ref[b * size : (b + 1) * size], keys, LAST)
        key_pos = lax.broadcasted_iota(jnp.int32, (1, raw.shape[1]), 1)
        query_pos = lax.broadcasted_iota(jnp.int32, (size, 1), 0) + b * size
        raw = jnp.where(key_pos < jnp.maximum(prefix, query_pos + 1), raw, -1e30)
        top = jnp.max(raw, axis=1, keepdims=True)
        expo = jnp.exp2((raw - top) * (score_scale * LOG2_E))
        total = jnp.sum(expo, axis=1, keepdims=True)
        out_ref[lax.bitwise_xor(place_ref[0], b), 0] = (dot(expo.astype(bf16), values) * (1.0 / total)).astype(bf16)


def probs_kernel(prefix_ref, hot_ref, table_ref, cos_ref, sin_ref, field_ref, probs_ref):
    prefix = prefix_ref[pl.program_id(0)]
    queries, keys, values = head_fields(hot_ref, table_ref, cos_ref, sin_ref)
    field_ref[0, 0, 0], field_ref[0, 0, 1], field_ref[0, 0, 2] = queries, keys, values
    _, _, blocks, _, size = probs_ref.shape
    for b in range(blocks):
        block = field_ref[0, 0, 0, b * size : (b + 1) * size]
        expo, total = softmax_columns(keys, block, b * size, prefix)
        probs_ref[0, 0, b] = (expo * (1.0 / total)).astype(bf16)


def attend_back_kernel(place_ref, field_ref, probs_ref, cos_ref, sin_ref, grad_ref, out_ref, key_sum, value_sum):
    head = pl.program_id(0)
    keys_t = field_ref[0, 0, 1].T
    values = field_ref[0, 0, 2]
    blocks, _, size, _ = grad_ref.shape
    width = out_ref.shape[-1] // 3

    def store(b, part, block):
        column = pl.multiple_of(part * width + head * HEAD, HEAD)
        out_ref[lax.bitwise_xor(place_ref[0], b), :, pl.ds(column, HEAD)] = block.astype(bf16)

    def unrotated(block, b):
        rows = slice(b * size, (b + 1) * size)
        block = block * score_scale
        return block * cos_ref[rows] - pltpu.roll(block, HEAD // 2, 1) * sin_ref[rows]

    for b in range(blocks):
        block = field_ref[0, 0, 0, b * size : (b + 1) * size]
        grad = grad_ref[b, 0]
        probs_low = probs_ref[0, 0, b]
        probs = probs_low.astype(f32)
        d_probs = dot(values, grad, LAST)
        inner = jnp.sum(probs * d_probs, axis=0, keepdims=True)
        d_scores = (probs * (d_probs - inner)).astype(bf16)
        key_part = dot(d_scores, block)
        value_part = dot(probs_low, grad)
        if b == 0:
            key_sum[...] = key_part
            value_sum[...] = value_part
        else:
            key_sum[...] += key_part
            value_sum[...] += value_part
        store(b, 0, unrotated(dot(keys_t, d_scores).T, b))
    for b in range(blocks):
        rows = slice(b * size, (b + 1) * size)
        store(b, 1, unrotated(key_sum[rows], b))
        store(b, 2, value_sum[rows])


def attention_specs(groups, size, vocab, twice):
    length = groups * size
    return [
        pl.BlockSpec(memory_space=pltpu.SMEM),
        pl.BlockSpec((groups, 1, size, vocab), lambda s, h: (0, s, 0, 0)),
        pl.BlockSpec((twice, 3, HEAD), lambda s, h: (0, 0, h)),
        pl.BlockSpec((length, HEAD), lambda s, h: (0, 0)),
        pl.BlockSpec((length, HEAD), lambda s, h: (0, 0)),
    ]


def attend(prefix, hot, table, cosine, sine):
    groups, seqs, size, vocab = hot.shape
    heads = table.shape[2] // HEAD
    length = groups * size
    return pl.pallas_call(
        attend_kernel,
        grid=(seqs, heads),
        in_specs=[pl.BlockSpec(memory_space=pltpu.SMEM)]
        + attention_specs(groups, size, vocab, table.shape[0]),
        out_specs=pl.BlockSpec((groups, 1, size, HEAD), lambda s, h: (0, s, 0, h)),
        out_shape=jax.ShapeDtypeStruct((groups, seqs, size, heads * HEAD), bf16),
        scratch_shapes=[pltpu.VMEM((length, HEAD), bf16)],
        compiler_params=pltpu.CompilerParams(vmem_limit_bytes=48 << 20),
        cost_estimate=pl.CostEstimate(
            flops=4 * seqs * heads * length * length * HEAD,
            bytes_accessed=4 * length * heads * HEAD * seqs,
            transcendentals=seqs * heads * length * length,
        ),
    )(place("seq"), prefix, hot, table, cosine, sine)


def probabilities(prefix, hot, table, cosine, sine):
    groups, seqs, size, vocab = hot.shape
    heads = table.shape[2] // HEAD
    length = groups * size
    return pl.pallas_call(
        probs_kernel,
        grid=(seqs, heads),
        in_specs=attention_specs(groups, size, vocab, table.shape[0]),
        out_specs=[
            pl.BlockSpec((1, 1, 3, length, HEAD), lambda s, h: (s, h, 0, 0, 0)),
            pl.BlockSpec((1, 1, groups, length, size), lambda s, h: (s, h, 0, 0, 0)),
        ],
        out_shape=[
            jax.ShapeDtypeStruct((seqs, heads, 3, length, HEAD), bf16),
            jax.ShapeDtypeStruct((seqs, heads, groups, length, size), bf16),
        ],
        compiler_params=pltpu.CompilerParams(vmem_limit_bytes=48 << 20),
        cost_estimate=pl.CostEstimate(
            flops=2 * seqs * heads * length * length * HEAD,
            bytes_accessed=2 * length * length * heads * seqs,
            transcendentals=seqs * heads * length * length,
        ),
    )(prefix, hot, table, cosine, sine)


def attend_back(s, fields, probs, cosine, sine, grad):
    groups, _, size, _ = grad.shape
    heads = fields.shape[1]
    length = groups * size
    return pl.pallas_call(
        attend_back_kernel,
        grid=(heads,),
        in_specs=[
            pl.BlockSpec(memory_space=pltpu.SMEM),
            pl.BlockSpec((1, 1, 3, length, HEAD), lambda h: (s, h, 0, 0, 0)),
            pl.BlockSpec((1, 1, groups, length, size), lambda h: (s, h, 0, 0, 0)),
            pl.BlockSpec((length, HEAD), lambda h: (0, 0)),
            pl.BlockSpec((length, HEAD), lambda h: (0, 0)),
            pl.BlockSpec((groups, 1, size, HEAD), lambda h: (0, s, 0, h)),
        ],
        out_specs=pl.BlockSpec((groups, size, 3 * heads * HEAD), lambda h: (0, 0, 0)),
        out_shape=jax.ShapeDtypeStruct((groups, size, 3 * heads * HEAD), bf16),
        scratch_shapes=[pltpu.VMEM((length, HEAD), f32), pltpu.VMEM((length, HEAD), f32)],
        compiler_params=pltpu.CompilerParams(vmem_limit_bytes=48 << 20),
        cost_estimate=pl.CostEstimate(
            flops=8 * heads * length * length * HEAD,
            bytes_accessed=2 * length * length * heads,
            transcendentals=0,
        ),
    )(place("seq"), fields, probs, cosine, sine, grad)


def on_device(
    token_ids,
    target_ids,
    prefix_lengths,
    cluster_ids,
    cluster_counts,
    embedding,
    qkv_weight,
    out_weight,
    norm1_gain,
    norm1_bias,
    gate_weight,
    up_weight,
    down_weight,
    norm2_gain,
    norm2_bias,
):
    seqs, local_len = token_ids.shape
    count = seqs * local_len
    groups = lax.axis_size("seq")
    dps = lax.axis_size("dp")
    devices = groups * dps
    seq_len = local_len * groups
    my_seq = lax.axis_index("seq")
    my_dp = lax.axis_index("dp")
    positions = my_seq * local_len + jnp.arange(local_len, dtype=jnp.int32)
    rows = qkv_weight.shape[0]
    width = embedding.shape[1]
    vocab_here = embedding.shape[0]
    vocab = vocab_here * devices
    hidden_units = gate_weight.shape[1]
    share = -(-hidden_units // (groups * LANES)) * LANES
    heads_here = HEADS // groups
    head_cols = heads_here * HEAD

    extra = jnp.concatenate(
        [norm1_gain, norm1_bias, norm2_gain, norm2_bias, token_ids.reshape(-1).astype(bf16)]
    )
    extra = jnp.pad(extra, (0, width - extra.shape[0])).reshape(1, width)
    pack = jnp.concatenate([embedding, extra], axis=0)
    chips = dps // 2
    packs = jnp.stack([pack] + [swap(pack, k) for k in range(1, groups)])
    qkv_blocks = swap_all(take_columns(qkv_weight, groups, 3, head_cols))
    packs = jnp.stack([packs] + [swap_dp(packs, 2 * j) for j in range(1, chips)])

    ff_weights = (gate_weight, up_weight, down_weight)
    ff_cols = jnp.concatenate([take_columns(weight, groups, 1, share) for weight in ff_weights], axis=2)
    ff_blocks = swap_all(ff_cols)
    out_mine, packs = together(out_weight, packs)
    packs = jnp.stack([packs, swap_dp(packs, 1)])
    qkv_cols = join_rows(qkv_blocks)
    out_blocks = jnp.stack([out_mine] + [swap_dp(out_mine, 2 * j) for j in range(1, chips)])

    owner = lax.bitwise_xor(my_dp, jnp.arange(2)[:, None] + 2 * jnp.arange(chips)[None, :])
    sender = owner[:, :, None] * groups + lax.bitwise_xor(my_seq, jnp.arange(groups))
    order = (jnp.arange(devices)[:, None] == sender.reshape(1, devices)).astype(bf16)
    packs = dot(order, packs.reshape(devices, (vocab_here + 1) * width)).reshape(devices, vocab_here + 1, width)
    embed_table = packs[:, :vocab_here].reshape(vocab, width).astype(bf16)
    extras = packs[:, vocab_here]
    norms = extras[:, : 4 * rows].reshape(devices, 4, rows)
    norms = norms.transpose(1, 0, 2).reshape(4, width)
    gain_one, bias_one, gain_two, bias_two = norms[0], norms[1], norms[2], norms[3]
    tokens_all = lax.dynamic_slice_in_dim(extras[:, 4 * rows : 4 * rows + count], my_dp * groups, groups, 0)
    tokens_all = tokens_all.astype(jnp.int32).reshape(groups, seqs, local_len)
    vocab_ids = jnp.arange(vocab, dtype=jnp.int32)
    token_hot = (token_ids.reshape(count)[:, None] == vocab_ids[None, :]).astype(bf16)

    piece = vocab // dps
    row_ids = (owner[:, :, None] * piece + jnp.arange(piece)).reshape(vocab).astype(jnp.int32)
    row_hot = (row_ids[:, None] == vocab_ids[None, :]).astype(bf16)
    all_hot = (tokens_all[..., None] == row_ids).astype(bf16)
    embed_dp = lax.dynamic_slice_in_dim(embed_table, my_dp * groups * rows, groups * rows, 1)
    embed_dp = dot(row_hot, embed_dp).astype(bf16)
    qkv_part = dot(embed_dp, qkv_cols)
    qkv_rows = sum_dp(qkv_part.reshape(2, chips, piece, 3 * head_cols), f32)

    qkv_rows, out_blocks = together(qkv_rows, out_blocks)
    qkv_table, chip_rows = spread_dp(halves(qkv_rows))
    qkv_table = qkv_table.transpose(2, 0, 1, 3, 4)

    ff_cols, qkv_cols, _ = together(join_rows(ff_blocks), qkv_cols, chip_rows)
    gate_w, up_w, down_w, qkv_w = (
        lax.all_gather(cols, "dp", axis=0, tiled=True)
        for cols in (*(ff_cols[:, i * share : (i + 1) * share] for i in range(3)), qkv_cols)
    )
    qkv_table = qkv_table.reshape(2 * vocab, 3, head_cols)
    angles = rotary_angles(jnp.arange(seq_len, dtype=jnp.int32), HEAD)
    cosine, sine = jnp.cos(angles), jnp.sin(angles)
    cosine = jnp.concatenate([cosine, cosine], axis=1)
    sine = jnp.concatenate([-sine, sine], axis=1)

    out_blocks, qkv_table = gather_blocks(out_blocks, qkv_table)
    contexts = []
    for s in range(seqs):
        context = attend(prefix_lengths[s : s + 1], all_hot[:, s : s + 1], qkv_table, cosine, sine)
        contexts.append(swap_all(context.reshape(groups, local_len, head_cols)))
    out_blocks, context = together(out_blocks, context)
    out_other = swap_dp(out_blocks, 1)
    context = join_lanes(contexts)
    out_full = join_out(out_blocks, out_other)

    inputs = dot(token_hot, embed_table)
    hidden, norm_one_pull = jax.vjp(
        layer_norm, deep_alpha * inputs + dot(context, out_full), gain_one, bias_one
    )

    def forward(k, block):
        values = gated_gelu(dot(block, gate_w), dot(block, up_w))
        return tuple(value.astype(bf16) for value in values)

    hidden_blocks, values, own_values = gather_tokens(
        hidden.astype(bf16), forward, lambda block: forward(0, block)
    )
    products, gate_slopes, up_slopes = zip(own_values, *values[1:])
    branch, _, (fields, probs) = scatter_tokens(
        lambda product: dot(product, down_w, LAST),
        products,
        None,
        lambda table: probabilities(prefix_lengths, all_hot, table, cosine, sine),
        (),
        (qkv_table,),
    )
    normed, norm_two_pull = jax.vjp(layer_norm, deep_alpha * hidden + branch, gain_two, bias_two)
    activations = normed.astype(bf16)

    logits = dot(activations, embed_table, LAST)
    cluster_hot = cluster_ids[:, None] == jnp.arange(cluster_counts.shape[0], dtype=jnp.int32)[None, :]
    members = jnp.sum(jnp.where(cluster_hot, cluster_counts[None, :], 0), axis=1).astype(f32)
    counted = (positions[None, :] >= prefix_lengths[:, None]).astype(f32)
    coefs = (
        loss_scale
        * (1.0 / members)[:, None]
        / (seq_len - prefix_lengths)[:, None].astype(f32)
        * counted
    )
    logit_exp = jnp.exp(logits - jnp.max(logits, axis=-1, keepdims=True))
    logit_probs = logit_exp / jnp.sum(logit_exp, axis=-1, keepdims=True)
    target_hot = (target_ids.reshape(count)[:, None] == vocab_ids[None, :]).astype(f32)
    d_logits = (coefs.reshape(count, 1) * (logit_probs - target_hot)).astype(bf16)
    head_grad = dot(d_logits, activations, ROWS)
    d_second, d_gain_two, d_bias_two = norm_two_pull(dot(d_logits, embed_table))

    d_second, qkv_w = together(d_second, qkv_w)

    def backward(k, block):
        d_product = dot(block, down_w)
        d_gate = (d_product * gate_slopes[k].astype(f32)).astype(bf16)
        d_up = (d_product * up_slopes[k].astype(f32)).astype(bf16)
        return d_gate, d_up

    def backward_own(block):
        d_gate, d_up = backward(0, block)
        parts = [
            dot(left, right, ROWS).astype(bf16)
            for left, right in ((hidden_blocks[0], d_gate), (hidden_blocks[0], d_up), (block, products[0]))
        ]
        return d_gate, d_up, dot(d_gate, gate_w, LAST) + dot(d_up, up_w, LAST), parts

    d_blocks, values, own_values = gather_tokens(d_second.astype(bf16), backward, backward_own)
    d_gates, d_ups = zip(own_values[:2], *values[1:])
    d_hidden_own, own_parts = own_values[2:]

    def weight_part(own_part, *blocks):
        rest = dot(jnp.concatenate(blocks[: groups - 1]), jnp.concatenate(blocks[groups - 1 :]), ROWS)
        return (own_part.astype(f32) + rest).astype(bf16)

    def last_parts(*values):
        return weight_part(*values[: 2 * groups - 1]), weight_part(*values[2 * groups - 1 :])

    def hidden_part(given):
        return dot(given[0], gate_w, LAST) + dot(given[1], up_w, LAST) if len(given) > 1 else given[0]

    d_hidden, gate_part, (up_part, down_part) = scatter_tokens(
        hidden_part,
        ((d_hidden_own,), *zip(d_gates[1:], d_ups[1:])),
        weight_part,
        last_parts,
        (own_parts[0], *hidden_blocks[1:], *d_gates[1:]),
        (own_parts[1], *hidden_blocks[1:], *d_ups[1:], own_parts[2], *d_blocks[1:], *products[1:]),
    )
    d_hidden = deep_alpha * d_second + d_hidden
    gate_rows, up_rows, down_rows = (
        lax.psum_scatter(part, "dp", scatter_dimension=0, tiled=True)
        for part in (gate_part, up_part, down_part)
    )

    d_first, d_gain_one, d_bias_one = norm_one_pull(d_hidden)
    d_attention = d_first.astype(bf16)
    d_context = dot(d_attention, out_full, LAST).astype(bf16)
    d_context = d_context.reshape(count, groups, head_cols).transpose(1, 0, 2)
    d_context = exchange(d_context, "seq").reshape(groups, seqs, local_len, head_cols)

    out_part = dot(context, d_attention, ROWS).astype(bf16)
    first_low = halves(d_first)
    lookup_first = dot(token_hot, first_low[0], ROWS) + dot(token_hot, first_low[1], ROWS)
    embed_part = head_grad + (lookup_scale * deep_alpha) * lookup_first
    d_context, out_part = together(d_context, out_part)
    out_rows = lax.psum_scatter(out_part, "dp", scatter_dimension=0, tiled=True)

    def own_rows(fields, *before):
        fields = together(fields, *before)[0]
        return swap_all(take_rows(fields, groups))

    d_qkv, input_blocks = [], []
    for s in range(seqs):
        grad = together(d_context, *input_blocks[-1][:1])[0] if s else d_context
        block = attend_back(s, fields, probs, cosine, sine, grad).reshape(seq_len, 3 * head_cols)
        part = dot(block, qkv_w, LAST).astype(bf16).reshape(groups, local_len, width)
        if s:
            part, input_blocks[-1] = together(part, input_blocks[-1])
        block, part = together(block, part)
        d_qkv.append(block)
        input_blocks.append(swap_all(part))

    tokens_near = jnp.stack(
        [lax.dynamic_index_in_dim(tokens_all, lax.bitwise_xor(my_seq, k), 0, False) for k in range(groups)]
    )
    near_hot = (tokens_near[..., None] == row_ids).astype(bf16)
    qkv_sums = sum(dot(near_hot[:, s].reshape(seq_len, vocab), d_qkv[s], ROWS) for s in range(seqs))
    sums_low = halves(qkv_sums)
    sums_low = jnp.stack([dot(row_hot, sums_low[0], ROWS), dot(row_hot, sums_low[1], ROWS)]).astype(bf16)
    lookup = dot(sums_low.reshape(2 * vocab, 3 * head_cols), qkv_w, LAST)
    embed_part = embed_part + lookup_scale * (lookup[:vocab] + lookup[vocab:])
    norm_part = halves(jnp.stack([d_gain_one, d_bias_one, d_gain_two, d_bias_two]))
    norm_part = norm_part.reshape(8, devices, rows).transpose(1, 0, 2).reshape(devices, 8 * rows)
    norm_part = jnp.pad(norm_part, ((0, 0), (0, width - 8 * rows))).reshape(devices, 1, width)
    small = embed_part.astype(bf16).reshape(devices, vocab_here, width)
    small = jnp.concatenate([small, norm_part], axis=1)
    sums_mine = sum_dp(qkv_sums.reshape(2, chips, piece, 3 * head_cols), bf16)
    small, _ = together(small, sums_mine)
    small = jnp.sum(exchange(small, BOTH).astype(f32), axis=0)
    embedding_grad = small[:vocab_here]
    norm_grads = small[vocab_here, : 8 * rows].reshape(2, 4, rows)
    norm_grads = norm_grads[0] + norm_grads[1]

    ff_blocks = own_rows([gate_rows, up_rows, down_rows], qkv_sums)
    sums_mine, input_blocks[-1], ff_blocks = together(sums_mine, input_blocks[-1], ff_blocks)
    input_grad = deep_alpha * d_first + jnp.concatenate(
        [sum(block.astype(f32) for block in blocks) for blocks in input_blocks]
    )
    sums_all = spread_dp(sums_mine.astype(bf16))[0].reshape(vocab, 3 * head_cols)
    qkv_rows = dot(embed_dp, sums_all, ROWS).astype(bf16)
    (qkv_grad,) = join_columns(own_rows([qkv_rows]), 3 * width, 3, 1)

    gate_grad, up_grad, down_grad = join_columns(ff_blocks, hidden_units, 1, 3)
    out_grad = sum(block.astype(f32) for block in own_rows([out_rows], sums_mine))

    return (
        activations.reshape(seqs, local_len, width),
        input_grad.reshape(seqs, local_len, width),
        embedding_grad,
        qkv_grad,
        out_grad,
        norm_grads[0],
        norm_grads[1],
        gate_grad,
        up_grad,
        down_grad,
        norm_grads[2],
        norm_grads[3],
    )


def solution(mesh):
    split = P(BOTH, None)
    line = P(BOTH)
    return jax.shard_map(
        on_device,
        mesh=mesh,
        in_specs=(
            P("dp", "seq"),
            P("dp", "seq"),
            P("dp"),
            P("dp"),
            P(),
            split,
            split,
            split,
            line,
            line,
            split,
            split,
            split,
            line,
            line,
        ),
        out_specs=(
            P("dp", "seq", None),
            P("dp", "seq", None),
            split,
            split,
            split,
            line,
            line,
            split,
            split,
            split,
            line,
            line,
        ),
        check_vma=False,
    )
```
